256 devices in a mesh: lat: 16 (over x, z_lo, core), lon: 16 (over y, z_hi).
Axes of the slice: x: 4, y: 4, z: 8 (z_hi: 4, z_lo: 2; z = z_hi * 2 + z_lo), core: 2. Of those that a mesh axis runs over, the one named last changes fastest.
Arguments:
- tracer_state: float32 [320, 1440, 128], P('lat', 'lon'), may hold values from 0.05 to 3
- limit_codes: int32 [2, 320, 1440], P(None, 'lat', 'lon'), may hold values from 0 to 4, as said below
- center_weight: float32 [320, 1440], P('lat', 'lon'), may hold values from 0.02 to 0.2
- side_weights: float32 [4, 320, 1440], P(None, 'lat', 'lon'), may hold values from 0.1 to 0.25
- growth: float32 [35], replicated, may hold values from 0.2 to 1
- half_sat: float32 [4, 35], replicated, may hold values from 0.1 to 1
- stoich: float32 [4, 35], replicated, may hold values from 0.0057142857 to 0.057142857
- mortality: float32 [35], replicated, may hold values from 0.05 to 0.3
- sinking: float32 [35], replicated, may hold values from 0.05 to 0.4
- routing: float32 [25, 35], replicated, may hold values from 0.0057142857 to 0.057142857
- remineral: float32 [25], replicated, may hold values from 0.02 to 0.3
- release: float32 [4, 25], replicated, may hold values from 0.008 to 0.08
- cotangent: float32 [320, 1440, 128], P('lat', 'lon'), may hold values from -0.5 to 1.5
Outputs:
- state_grad: float32 [320, 1440, 128], P('lat', 'lon')
- growth_grad: float32 [35], replicated
The draws below stay inside these ranges and needn't reach their ends.
Inputs may be any that keep to these rules, and one draw needn't show every extreme that they name: `limit_codes`: 4 marks a dry cell, the same cells on every level; otherwise the code names the nutrient (0 nitrate, 1 phosphate, 2 iron, 3 silicate) that limits growth in that cell and level. The dry share differs from one device block of 20 x 90 cells to another.
All inputs are finite; a program needn't handle non-finite values.
Results may differ from the reference program's by a relative error of at most 0.0003.
Values sent between devices are 32-bit elements; how exact they have to be, the bound alone decides.
A program may use at most 64 MiB of HBM per device.

```python
import math
import jax
import jax.numpy as jnp
from jax import lax

TRACERS = 64
PHYTO = 35
NUTRIENTS = 4
LEVELS = 2
SUBSTEPS = 4
ROWS_DEV = 20
COLS_DEV = 90
ORGANIC = 25
CHANNELS = 128
ROWS = 320
COLS = 1440
N_LAT = 16


def draw_limit_codes(key, part):
    key = jax.random.fold_in(key, 7)
    tile_key, cell_key, nutrient_key = jax.random.split(key, 3)
    bands = ROWS // ROWS_DEV
    sectors = COLS // COLS_DEV
    tile_level = jax.random.randint(tile_key, (bands, sectors), 0, 5)
    tile_level = jnp.repeat(jnp.repeat(tile_level, ROWS_DEV, axis=0), COLS_DEV, axis=1)
    cell_level = jax.random.randint(cell_key, (ROWS, COLS), 0, 6)
    dry_cell = cell_level < tile_level
    nutrient_code = jax.random.randint(nutrient_key, (LEVELS, ROWS, COLS), 0, 4)
    return jnp.where(dry_cell[None], 4, nutrient_code).astype(jnp.int32)


def steps_of(key, shape, shards, least, largest):
    factor_of = 1.0
    for dim, blocks in shards:
        steps = jax.random.uniform(jax.random.fold_in(jax.random.fold_in(key, 6), dim), (blocks,), jnp.float32, least / len(shards), largest / len(shards))
        factor_of = factor_of * jnp.repeat(jnp.exp(steps), shape[dim] // blocks).reshape((-1,) + (1,) * (len(shape) - 1 - dim))
    return factor_of


def setup_inputs(seed: int = 0) -> dict:
    splits = jax.random.split(jax.random.key(seed), 14)
    tracer_state = jnp.clip(jnp.exp(math.log(3.0) - 4.0943445 * jax.random.uniform(splits[0], (ROWS, COLS, CHANNELS), jnp.float32) ** steps_of(splits[0], (ROWS, COLS, CHANNELS), ((0, 16), (1, 16)), -0.2, 0.2)), 0.05, 3.0)
    limit_codes = draw_limit_codes(jax.random.fold_in(splits[13], 71), 0)
    center_weight = jnp.clip(0.02 + 0.18 * jax.random.uniform(splits[2], (ROWS, COLS), jnp.float32) ** steps_of(splits[2], (ROWS, COLS), ((0, 16), (1, 16)), -0.2, 0.2), 0.02, 0.2)
    side_weights = jnp.clip(0.1 + 0.15 * jax.random.uniform(splits[3], (4, ROWS, COLS), jnp.float32) ** steps_of(splits[3], (4, ROWS, COLS), ((1, 16), (2, 16)), -0.2, 0.2), 0.1, 0.25)
    growth = jnp.clip(jnp.exp(jax.random.uniform(splits[4], (PHYTO,), jnp.float32, math.log(0.2), math.log(1.0))), 0.2, 1.0)
    half_sat = jnp.clip(jnp.exp(jax.random.uniform(splits[5], (NUTRIENTS, PHYTO), jnp.float32, math.log(0.1), math.log(1.0))), 0.1, 1.0)
    stoich = jnp.clip(jnp.exp(jax.random.uniform(splits[6], (NUTRIENTS, PHYTO), jnp.float32, math.log(0.0057142857), math.log(0.057142857))), 0.0057142857, 0.057142857)
    mortality = jnp.clip(jnp.exp(jax.random.uniform(splits[7], (PHYTO,), jnp.float32, math.log(0.05), math.log(0.3))), 0.05, 0.3)
    sinking = jnp.clip(jnp.exp(jax.random.uniform(splits[8], (PHYTO,), jnp.float32, math.log(0.05), math.log(0.4))), 0.05, 0.4)
    routing = jnp.clip(jnp.exp(jax.random.uniform(splits[9], (ORGANIC, PHYTO), jnp.float32, math.log(0.0057142857), math.log(0.057142857))), 0.0057142857, 0.057142857)
    remineral = jnp.clip(jnp.exp(jax.random.uniform(splits[10], (ORGANIC,), jnp.float32, math.log(0.02), math.log(0.3))), 0.02, 0.3)
    release = jnp.clip(jnp.exp(jax.random.uniform(splits[11], (NUTRIENTS, ORGANIC), jnp.float32, math.log(0.008), math.log(0.08))), 0.008, 0.08)
    cotangent = jnp.clip(-0.5 + 2.0 * jax.random.uniform(splits[12], (ROWS, COLS, CHANNELS), jnp.float32) ** steps_of(splits[12], (ROWS, COLS, CHANNELS), ((0, 16), (1, 16)), -0.2, 0.2), -0.5, 1.5)
    return dict(tracer_state=tracer_state, limit_codes=limit_codes, center_weight=center_weight, side_weights=side_weights, growth=growth, half_sat=half_sat, stoich=stoich, mortality=mortality, sinking=sinking, routing=routing, remineral=remineral, release=release, cotangent=cotangent)


def biology(tracer_field, limit_codes, growth, half_sat, stoich, mortality, sinking, routing, remineral, release):
    height, breadth = (tracer_field.shape[0], tracer_field.shape[1])
    tracers = tracer_field.reshape(height, breadth, LEVELS, TRACERS)
    nutrient = tracers[..., :NUTRIENTS]
    phyto_pool = tracers[..., NUTRIENTS:NUTRIENTS + PHYTO]
    organic = tracers[..., NUTRIENTS + PHYTO:]
    chosen = (jnp.moveaxis(limit_codes, 0, 2)[..., None] == jnp.arange(NUTRIENTS, dtype=jnp.int32)).astype(jnp.float32)
    wet_share = lax.optimization_barrier(jnp.sum(chosen, axis=3))
    picked = lax.optimization_barrier(jnp.sum(chosen * nutrient, axis=3))
    picked_half = jnp.einsum('hblk,kp->hblp', chosen, half_sat, precision=lax.Precision.HIGHEST)
    limitation = picked[..., None] / (picked[..., None] + picked_half + (1.0 - wet_share)[..., None])
    light_level = 0.4 ** jnp.arange(LEVELS, dtype=jnp.float32)
    uptake = growth * light_level[:, None] * limitation * phyto_pool
    mortal_loss = mortality * phyto_pool
    grown_phyto = phyto_pool + uptake - mortal_loss
    falling = sinking * grown_phyto
    from_above = jnp.concatenate([jnp.zeros_like(falling[:, :, :1]), falling[:, :, :-1]], axis=2)
    decay_flux = remineral * organic
    nutrient_new = nutrient - jnp.einsum('hblp,kp->hblk', uptake, stoich, precision=lax.Precision.HIGHEST)
    nutrient_new = nutrient_new + jnp.einsum('hblr,kr->hblk', decay_flux, release, precision=lax.Precision.HIGHEST)
    organic_new = organic + jnp.einsum('hblp,rp->hblr', mortal_loss, routing, precision=lax.Precision.HIGHEST) - decay_flux
    outcome = jnp.concatenate([nutrient_new, grown_phyto - falling + from_above, organic_new], axis=3)
    return outcome.reshape(height, breadth, LEVELS * TRACERS)

def advance(padded, center, sides, wet_channels):
    middle = padded[1:-1, 1:-1]
    summed = center[..., None] * middle + sides[0][..., None] * padded[1:-1, 2:]
    summed = summed + sides[1][..., None] * padded[1:-1, :-2]
    summed = summed + sides[2][..., None] * padded[2:, 1:-1] + sides[3][..., None] * padded[:-2, 1:-1]
    return wet_channels * summed

def channel_mask(limit_codes):
    wet_mask = (limit_codes != 4).astype(jnp.float32)
    return jnp.repeat(jnp.moveaxis(wet_mask, 0, 2), TRACERS, axis=2)

def step_forward(tracer_state, limit_codes, center_weight, side_weights, growth, half_sat, stoich, mortality, sinking, routing, remineral, release):
    wet_channels = channel_mask(limit_codes)
    moved = tracer_state * wet_channels
    for step_index in range(SUBSTEPS):
        moved = advance(jnp.pad(moved, ((1, 1), (1, 1), (0, 0))), center_weight, side_weights, wet_channels)
    return biology(moved, limit_codes, growth, half_sat, stoich, mortality, sinking, routing, remineral, release)

def reference(tracer_state, limit_codes, center_weight, side_weights, growth, half_sat, stoich, mortality, sinking, routing, remineral, release, cotangent):
    reach = 2 * SUBSTEPS
    window = ROWS_DEV + 2 * reach
    state_pad = jnp.pad(tracer_state, ((reach, reach), (0, 0), (0, 0)))
    cot_pad = jnp.pad(cotangent, ((reach, reach), (0, 0), (0, 0)))
    codes_pad = jnp.pad(limit_codes, ((0, 0), (reach, reach), (0, 0)), constant_values=4)
    center_pad = jnp.pad(center_weight, ((reach, reach), (0, 0)))
    sides_pad = jnp.pad(side_weights, ((0, 0), (reach, reach), (0, 0)))
    offsets = jnp.arange(window, dtype=jnp.int32)
    mask_wide = ((offsets >= reach - SUBSTEPS) & (offsets < reach + ROWS_DEV + SUBSTEPS)).astype(jnp.float32)[:, None, None]
    mask_own = ((offsets >= reach) & (offsets < reach + ROWS_DEV)).astype(jnp.float32)[:, None, None]

    def window_pass(block_index):
        first = (block_index * ROWS_DEV).astype(jnp.int32)
        state_win = lax.dynamic_slice_in_dim(state_pad, first, window, 0)
        cot_win = lax.dynamic_slice_in_dim(cot_pad, first, window, 0)
        codes_win = lax.dynamic_slice_in_dim(codes_pad, first, window, 1)
        center_win = lax.dynamic_slice_in_dim(center_pad, first, window, 0)
        sides_win = lax.dynamic_slice_in_dim(sides_pad, first, window, 1)

        def local_step(moved, rates):
            return step_forward(moved, codes_win, center_win, sides_win, rates, half_sat, stoich, mortality, sinking, routing, remineral, release)
        outcome, pullback = jax.vjp(local_step, state_win, growth)
        state_bar = pullback(cot_win * mask_wide)[0]
        growth_bar = pullback(cot_win * mask_own)[1]
        return (state_bar[reach:reach + ROWS_DEV], growth_bar)
    blocks, growth_parts = lax.map(window_pass, jnp.arange(N_LAT, dtype=jnp.int32))
    state_grad = blocks.reshape(ROWS, COLS, LEVELS * TRACERS)
    growth_grad = lax.optimization_barrier(jnp.sum(growth_parts, axis=0)) / (ROWS * COLS * LEVELS)
    return (state_grad, growth_grad)
```

```python
import jax
import jax.numpy as jnp
from jax import lax
from jax.experimental import pallas as pl
from jax.experimental.pallas import tpu as pltpu
from jax.sharding import PartitionSpec as P

TRACERS = 64
PHYTO = 35
NUTRIENTS = 4
ORGANIC = 25
LEVELS = 2
SUBSTEPS = 4
ROWS_DEV = 20
COLS_DEV = 90
CHANNELS = 128
FIRST_P = NUTRIENTS
FIRST_O = NUTRIENTS + PHYTO


HALO = SUBSTEPS
ALL_ROWS = ROWS_DEV + 2 * HALO
BLOCKS = 13
COLS_PAD = 8 * BLOCKS
LEFT = 8
RIGHT = LEFT + COLS_DEV
ROW = (BLOCKS, 8, CHANNELS)
GROUP = 4
GROUPS = ROWS_DEV // GROUP
GROUP_CELLS = GROUP * COLS_PAD
KINDS = 6
CODES = NUTRIENTS + 1
CELLS = 320 * 1440 * LEVELS
MESH = pl.DeviceIdType.MESH
SENT = (3, 2, 3)
MOVES = ((-1, 0), (1, 0), (0, -1), (0, 1), (-1, -1), (-1, 1), (1, -1), (1, 1))
INNER_LOOPS = (0, 3, 2, 2, 2)
RADIX = 4
NEAR = RADIX * RADIX
F32 = jnp.float32
BF16 = jnp.bfloat16


def split(value):
    high = value.astype(BF16)
    low = (value - high.astype(F32)).astype(BF16)
    return jnp.concatenate([high, low], axis=1)


def dot(a, b):
    return jnp.dot(a, b, preferred_element_type=F32)


def cell(column):
    return column % BLOCKS, column // BLOCKS


def blocked(jj):
    return pl.ds(jj, 8, stride=BLOCKS)


def forward_block(weights, dst, src, i, count):
    above = [src[i - 1, jj] for jj in range(BLOCKS)]
    rows = [[src[i + d, jj] for jj in range(BLOCKS)] for d in range(count)]
    under = [src[i + count, jj] for jj in range(BLOCKS)]
    rows = [above] + rows + [under]
    for jj in range(BLOCKS):
        for d in range(count):
            row = rows[d + 1]
            east = row[jj + 1] if jj < BLOCKS - 1 else pltpu.roll(row[0], 7, 0)
            west = row[jj - 1] if jj > 0 else pltpu.roll(row[BLOCKS - 1], 1, 0)
            total = weights[0, i + d, jj] * row[jj]
            total += weights[1, i + d, jj] * east
            total += weights[2, i + d, jj] * west
            total += weights[3, i + d, jj] * rows[d + 2][jj]
            total += weights[4, i + d, jj] * rows[d][jj]
            dst[i + d, jj] = total


def backward_block(weights, put, src, i, count):
    rows = [[src[i + d, jj] for jj in range(BLOCKS)] for d in range(-1, count + 1)]
    for jj in range(BLOCKS):
        for d in range(count):
            row = rows[d + 1]
            if jj > 0:
                from_west = weights[1, i + d, jj - 1] * row[jj - 1]
            else:
                from_west = pltpu.roll(weights[1, i + d, BLOCKS - 1] * row[BLOCKS - 1], 1, 0)
            if jj < BLOCKS - 1:
                from_east = weights[2, i + d, jj + 1] * row[jj + 1]
            else:
                from_east = pltpu.roll(weights[2, i + d, 0] * row[0], 7, 0)
            total = weights[0, i + d, jj] * row[jj]
            total += weights[3, i + d - 1, jj] * rows[d][jj]
            total += weights[4, i + d + 1, jj] * rows[d + 2][jj]
            put(i + d, jj, total + (from_west + from_east))


def outer_rows(block, weights, to, src, step):
    block(weights, to, src, step, HALO)
    block(weights, to, src, ALL_ROWS - HALO - step, HALO)


def into(dst):
    def put(i, jj, total):
        dst[i, jj] = total

    return put


def kernel(
    state_hbm,
    cot_hbm,
    codes_hbm,
    center_hbm,
    sides_hbm,
    growth_hbm,
    mortality_hbm,
    sinking_hbm,
    remineral_hbm,
    half_sat_hbm,
    stoich_hbm,
    routing_hbm,
    release_hbm,
    result,
    totals,
    state,
    cot,
    codes,
    center,
    sides,
    growth,
    mortality,
    sinking,
    remineral,
    half_sat,
    stoich,
    routing,
    release,
    kinds,
    kinds_t,
    vectors,
    pieces,
    hot,
    halves,
    carried,
    parts,
    bar0,
    drive,
    picked,
    pull,
    weights,
    v,
    b,
    acc,
    row_out,
    row_in,
    col_out,
    col_in,
    corner_out,
    corner_in,
    gather,
    load_sem,
    send_sem,
    recv_sem,
    gsend_sem,
    grecv_sem,
):
    lat, lon = lax.axis_index("lat"), lax.axis_index("lon")
    n_lat, n_lon = lax.axis_size("lat"), lax.axis_size("lon")

    def there(move):
        i, j = lat + move[0], lon + move[1]
        return (i >= 0) & (i < n_lat) & (j >= 0) & (j < n_lon)

    def back(move):
        return there((-move[0], -move[1]))

    lat_low, lat_high = lax.rem(lat, RADIX), lax.div(lat, RADIX)
    lon_low, lon_high = lax.rem(lon, RADIX), lax.div(lon, RADIX)
    places = (lat_high * RADIX + lon_high, lat_low * RADIX + lon_low)

    def peer(stage, turn):
        index = lax.rem(places[stage] + turn, NEAR)
        high, low = lax.div(index, RADIX), lax.rem(index, RADIX)
        if stage == 0:
            return index, (high * RADIX + lat_low, low * RADIX + lon_low)
        return index, (lat_high * RADIX + high, lon_high * RADIX + low)

    inner = pl.ds(LEFT, COLS_DEV)
    sources = (
        (codes_hbm, codes),
        (center_hbm, center),
        (sides_hbm, sides),
        (state_hbm, state.at[:, inner, :]),
        (cot_hbm, cot.at[:, inner, :]),
        (growth_hbm, growth),
        (mortality_hbm, mortality),
        (sinking_hbm, sinking),
        (remineral_hbm, remineral),
        (half_sat_hbm, half_sat),
        (stoich_hbm, stoich),
        (routing_hbm, routing),
        (release_hbm, release),
    )
    loads = [
        pltpu.make_async_copy(source, target, load_sem.at[n])
        for n, (source, target) in enumerate(sources)
    ]
    for load in loads:
        load.start()

    barrier = pltpu.get_barrier_semaphore()
    count = jnp.int32(2 * (NEAR - 1))
    for move in MOVES:
        near = there(move)
        count = count + near.astype(jnp.int32)

        @pl.when(near)
        def _():
            pl.semaphore_signal(
                barrier, inc=1, device_id=(lat + move[0], lon + move[1]), device_id_type=MESH
            )

    for stage in range(2):

        @pl.loop(1, NEAR)
        def _(turn):
            pl.semaphore_signal(
                barrier, inc=1, device_id=peer(stage, turn)[1], device_id_type=MESH
            )

    for which, move in enumerate(MOVES):

        @pl.when(jnp.logical_not(back(move)))
        def _():
            for phase in range(3):
                if which < 2:
                    for r in range(SENT[phase]):
                        row_in[phase, which, r, LEFT:RIGHT] = jnp.zeros((COLS_DEV, CHANNELS), F32)
                elif which < 4:
                    col_in[phase, which - 2] = jnp.zeros_like(col_in[phase, which - 2])
                elif phase != 1:
                    corner_in[phase, which - 4] = jnp.zeros_like(corner_in[phase, which - 4])

    left_zeros = jnp.zeros((LEFT, CHANNELS), F32)
    right_zeros = jnp.zeros((COLS_PAD - RIGHT, CHANNELS), F32)

    @pl.loop(0, ROWS_DEV)
    def _(i):
        state[i, 0:LEFT] = left_zeros
        state[i, RIGHT:COLS_PAD] = right_zeros
        cot[i, 0:LEFT] = left_zeros
        cot[i, RIGHT:COLS_PAD] = right_zeros

    for phase in range(3):
        for which in range(2):
            for r in range(SENT[phase]):
                row_in[phase, which, r, 0:LEFT] = left_zeros
                row_in[phase, which, r, RIGHT:COLS_PAD] = right_zeros
    corner_out[...] = jnp.zeros_like(corner_out)

    kinds[...] = jnp.zeros_like(kinds)
    kinds_t[...] = jnp.zeros_like(kinds_t)
    for load in loads[:3]:
        load.wait()
    upper_code, lower_code = codes[:, 0, :], codes[:, 1, :]
    wet = (upper_code != NUTRIENTS).astype(F32)
    every = lambda k: pl.ds(k, ROWS_DEV, stride=KINDS)
    kinds[every(0), 0:COLS_DEV] = wet * center[...]
    for s in range(4):
        kinds[every(s + 1), 0:COLS_DEV] = wet * sides[:, s, :]
    kinds[every(5), 0:COLS_DEV] = (upper_code + CODES * lower_code).astype(F32)
    kinds_t[LEFT:RIGHT] = kinds[...].T[0:COLS_DEV]

    lane = lax.broadcasted_iota(jnp.int32, (1, CHANNELS), 1)
    lane_in = lax.rem(lane, TRACERS)
    organic = lane_in >= FIRST_O
    loads[3].wait()

    def carry(i, low, high):
        turned = pltpu.roll(kinds_t[low:high], (FIRST_O - KINDS * i) % CHANNELS, 1)
        wide = jnp.broadcast_to(turned[:, FIRST_O : FIRST_O + 1], (high - low, CHANNELS))
        masked = jnp.where(wide > 0, state[i, low:high], 0.0)
        state[i, low:high] = jnp.where(organic, turned, masked)

    for i in range(ROWS_DEV):
        if i < HALO or i >= ROWS_DEV - HALO:
            carry(i, 0, COLS_PAD)
        else:
            carry(i, LEFT, LEFT + 8)
            carry(i, 88, COLS_PAD)

    lane_free = lane_in >= FIRST_O + 5

    def turn_by(value, shift):
        return pltpu.roll(value, shift % CHANNELS, 1)

    def pack_state(cells):
        return [
            jnp.where(lane_free, turn_by(cells[3], FIRST_O + 5 - 20 * n), cells[n]) for n in range(3)
        ]

    def unpack_state(sent_cells):
        last = [turn_by(sent_cells[n], 20 * n - FIRST_O - 5) for n in range(3)]
        last = jnp.where(lane_in < 20, last[0], jnp.where(lane_in < 40, last[1], last[2]))
        return list(sent_cells) + [last]

    def pack_organic(cells):
        return [jnp.where(organic, cells[n], turn_by(cells[n + 2], -FIRST_O)) for n in range(2)]

    def pack_bars(cells):
        return [
            jnp.where(organic, turn_by(cells[3], FIRST_O), cells[0]),
            jnp.where(organic, turn_by(cells[3], FIRST_O - ORGANIC), cells[1]),
            cells[2],
        ]

    def unpack_bars(sent_cells, sent_organic):
        last = jnp.where(
            lane_in < ORGANIC,
            turn_by(sent_cells[0], -FIRST_O),
            turn_by(sent_cells[1], ORGANIC - FIRST_O),
        )
        others = list(sent_organic) + [turn_by(cells, FIRST_O) for cells in sent_organic]
        return [
            jnp.where(organic, other, cells)
            for other, cells in zip(others, list(sent_cells) + [last])
        ]

    def received_cols(phase, side):
        cells = [col_in[phase, side, n] for n in range(3)]
        if phase == 0:
            return unpack_state(cells)
        return unpack_bars(cells, [col_in[1, side, n] for n in range(2)])

    def received_rows(phase, which, jj):
        cells = [row_in[phase, which, n, blocked(jj), :] for n in range(3)]
        if phase == 0:
            return unpack_state(cells)
        return unpack_bars(cells, [row_in[1, which, n, blocked(jj), :] for n in range(2)])

    def message(phase, which):
        move = MOVES[which]
        sent_rows = pl.ds(0, SENT[phase])
        if which < 2:
            source = row_out.at[phase, which, sent_rows, inner, :]
            target = row_in.at[phase, which, sent_rows, inner, :]
        elif which < 4:
            source = col_out.at[phase, which - 2, sent_rows]
            target = col_in.at[phase, which - 2, sent_rows]
        else:
            source, target = corner_out.at[phase, which - 4], corner_in.at[phase, which - 4]
        return pltpu.make_async_remote_copy(
            src_ref=source,
            dst_ref=target,
            send_sem=send_sem.at[phase, which],
            recv_sem=recv_sem.at[phase, which],
            device_id=(lat + move[0], lon + move[1]),
            device_id_type=MESH,
        )

    def send(phase, which):
        @pl.when(there(MOVES[which]))
        def _():
            message(phase, which).start()

    def sent(phase, which):
        @pl.when(there(MOVES[which]))
        def _():
            message(phase, which).wait_send()

    def arrived(phase, which):
        @pl.when(back(MOVES[which]))
        def _():
            message(phase, which).wait_recv()

    def corner_cells(which, inside):
        down, right = MOVES[4 + which]
        at = 0
        for depth in range(3):
            for t in range(3 - depth):
                if inside:
                    row = depth if down < 0 else ROWS_DEV - 1 - depth
                    column = LEFT + t if right < 0 else RIGHT - 1 - t
                else:
                    row = ROWS_DEV + depth if down < 0 else -1 - depth
                    column = RIGHT + t if right < 0 else LEFT - 1 - t
                yield at, row, column
                at += 1

    weight_cells = weights.reshape(5 * ALL_ROWS * COLS_PAD, CHANNELS)

    def column_cells(jj, s, base=0):
        return pl.ds(base + HALO * COLS_PAD + 8 * jj + s, ROWS_DEV, stride=COLS_PAD)

    def unpack_cols(phase, field):
        cells = field.reshape(ALL_ROWS * COLS_PAD, CHANNELS)
        for side in range(2):
            halo = received_cols(phase, side)
            for t in range(HALO):
                jj, s = cell(RIGHT + t if side == 0 else LEFT - HALO + t)
                cells[column_cells(jj, s), :] = halo[t]
                for k in range(5 if phase == 0 else 0):
                    weight_cells[column_cells(jj, s, k * ALL_ROWS * COLS_PAD), :] = (
                        jnp.broadcast_to(
                            halo[t][:, FIRST_O + k : FIRST_O + k + 1], (ROWS_DEV, CHANNELS)
                        )
                    )

    def unpack_rows(phase, field):
        for which in range(2):
            first = ALL_ROWS - HALO if which == 0 else 0
            for jj in range(BLOCKS):
                for r, cells in enumerate(received_rows(phase, which, jj)):
                    field[first + r, jj] = cells

        for which in range(4):
            for at, row, column in corner_cells(which, False):
                jj, s = cell(column)
                field[HALO + row, jj, s : s + 1, :] = corner_in[phase, which, at : at + 1, :]

    state_cells = state.reshape(ROWS_DEV * COLS_PAD, CHANNELS)
    for side in range(2):
        at = LEFT if side == 0 else RIGHT - HALO
        cells = [state_cells[pl.ds(at + t, ROWS_DEV, stride=COLS_PAD), :] for t in range(HALO)]
        for n, value in enumerate(pack_state(cells)):
            col_out[0, side, n] = value
    for which in range(2):
        first = 0 if which == 0 else ROWS_DEV - HALO
        for n, value in enumerate(pack_state([state[first + r] for r in range(HALO)])):
            row_out[0, which, n] = value

    for which in range(4):
        for at, row, column in corner_cells(which, True):
            corner_out[0, which, at : at + 1] = state[row, column : column + 1]

    order = (2, 3, 0, 1, 4, 5, 6, 7)
    pl.semaphore_wait(barrier, count)
    for which in order:
        send(0, which)

    v0 = v.at[0]

    lane_f = lane_in.astype(F32)
    upper = lane < TRACERS

    for load in loads[5:]:
        load.wait()
    vectors[...] = jnp.zeros_like(vectors)
    pieces[...] = jnp.zeros_like(pieces)
    for l in range(LEVELS):
        n, p, o = l * TRACERS, l * TRACERS + FIRST_P, l * TRACERS + FIRST_O
        end = (l + 1) * TRACERS
        vectors[0:1, p:o] = growth[...]
        vectors[1:2, p:o] = mortality[...]
        vectors[2:3, p:o] = sinking[...]
        vectors[3:4, o:end] = remineral[...]
        pieces[0, n : n + NUTRIENTS, p:o] = stoich[...]
        pieces[1, o:end, p:o] = routing[...]
        pieces[2, n : n + NUTRIENTS, o:end] = release[...]
        pieces[3, n : n + NUTRIENTS, p:o] = half_sat[...]
    rate, lost, sunk, decayed = (vectors[n : n + 1, :] for n in range(4))

    row_lane = lax.broadcasted_iota(jnp.int32, (CHANNELS, CHANNELS), 0)
    col_lane = lax.broadcasted_iota(jnp.int32, (CHANNELS, CHANNELS), 1)
    same = (row_lane < TRACERS) == (col_lane < TRACERS)
    row_in_level = lax.rem(row_lane, TRACERS)
    col_in_level = lax.rem(col_lane, TRACERS)
    row_p = (row_in_level >= FIRST_P) & (row_in_level < FIRST_O)
    col_p = (col_in_level >= FIRST_P) & (col_in_level < FIRST_O)
    own = jnp.where(row_lane == col_lane, 1.0, 0.0)
    own_p = jnp.where((row_lane == col_lane) & col_p, 1.0, 0.0)
    below = jnp.where(row_lane == col_lane + TRACERS, 1.0, 0.0)
    bars = own * ((1.0 - lost) * (1.0 - sunk) * (1.0 - decayed))
    bars += below * ((1.0 - lost) * sunk) + pieces[1] * lost + pieces[2] * decayed
    light = jnp.where(upper, 1.0, 0.4)
    drives = light * (own_p * (1.0 - sunk) + below * sunk - pieces[0])
    ones = jnp.where(col_p[0:1], 0.0, 1.0)
    halves_of = [pieces[3, k : k + 1, :] + pieces[3, TRACERS + k : TRACERS + k + 1, :] + ones for k in range(NUTRIENTS)]
    pick = jnp.where(same & (row_in_level < NUTRIENTS) & col_p, 1.0, 0.0).astype(BF16)
    collect = jnp.where(same & (col_in_level < NUTRIENTS) & row_p, 1.0, 0.0).astype(BF16)
    pick = jnp.concatenate([pick, pick], axis=0)
    collect = jnp.concatenate([collect, collect], axis=0)
    maps = jnp.concatenate([bars, drives], axis=1)
    maps_high = maps.astype(BF16)
    maps_low = (maps - maps_high.astype(F32)).astype(BF16)
    maps_twice = jnp.concatenate([maps_high, maps_high], axis=0)

    for i in range(HALO, ROWS_DEV - HALO):
        turned = pltpu.roll(kinds_t[16:88], (FIRST_O - KINDS * i) % CHANNELS, 1)
        state[i, 16:88] = jnp.where(organic, turned, state[i, 16:88])
    spread = jnp.concatenate(
        [jnp.where(row_lane == FIRST_O + k, 1.0, 0.0).astype(BF16) for k in range(5)], axis=1
    )
    spread = jnp.concatenate([spread, spread], axis=0)
    for n in range(ROWS_DEV // 2):
        block = jnp.concatenate(
            [state[2 * n + r, blocked(jj), :] for r in range(2) for jj in range(BLOCKS)], axis=0
        )
        carried[2 * COLS_PAD * n : 2 * COLS_PAD * (n + 1)] = split(block)
    for g in range(GROUPS):
        cells = pl.ds(GROUP_CELLS * g, GROUP_CELLS)
        wide = dot(carried[cells], spread)
        for k in range(5):
            part = wide[:, CHANNELS * k : CHANNELS * (k + 1)]
            weights[k, HALO + GROUP * g : HALO + GROUP * (g + 1)] = part.reshape((GROUP,) + ROW)
        for i in range(GROUP * g, GROUP * (g + 1)):
            for jj in range(BLOCKS):
                cells = state[i, blocked(jj), :]
                v0[HALO + i, jj] = jnp.where(weights[0, HALO + i, jj] > 0, cells, 0.0)
                code = jnp.broadcast_to(cells[:, FIRST_O + 5 : FIRST_O + 6], (8, CHANNELS))
                second = jnp.floor((code + 0.5) * (1.0 / CODES))
                here = jnp.where(upper, code - CODES * second, second)
                hot[i, jj] = jnp.where(here == lane_f, 1.0, 0.0)
                halved = jnp.ones((8, CHANNELS), F32)
                for k in range(NUTRIENTS):
                    halved = jnp.where(here == k, halves_of[k], halved)
                halves[i, jj] = halved

    loads[4].wait()
    for n in range(ROWS_DEV // 2):
        block = jnp.concatenate(
            [cot[2 * n + r, blocked(jj), :] for r in range(2) for jj in range(BLOCKS)], axis=0
        )
        parts[2 * COLS_PAD * n : 2 * COLS_PAD * (n + 1)] = split(block)
    for n in range(GROUPS):
        cells = pl.ds(GROUP_CELLS * n, GROUP_CELLS)
        both = dot(parts[cells], maps_twice) + dot(parts[cells, 0:CHANNELS], maps_low)
        bar0[cells] = both[:, :CHANNELS]
        drive[cells] = both[:, CHANNELS:]

    for side in range(2):
        cells = []
        for t in range(HALO):
            jj, s = cell(LEFT + t if side == 0 else RIGHT - HALO + t)
            cells.append(bar0[pl.ds(8 * jj + s, ROWS_DEV, stride=COLS_PAD), :])
        for n, value in enumerate(pack_organic(cells)):
            col_out[1, side, n] = value
    for which in range(2):
        first = 0 if which == 0 else ROWS_DEV - HALO
        for jj in range(BLOCKS):
            cells = [
                bar0[COLS_PAD * (first + r) + 8 * jj : COLS_PAD * (first + r) + 8 * jj + 8]
                for r in range(HALO)
            ]
            for n, value in enumerate(pack_organic(cells)):
                row_out[1, which, n, blocked(jj), :] = value
    for which in range(4):
        send(1, which)

    def inner_rows(block, to, src, step):
        count = (ROWS_DEV - 2 * step) // INNER_LOOPS[step]

        @pl.loop(0, INNER_LOOPS[step])
        def _(n):
            block(weights, to, src, HALO + step + count * n, count)

    one = (COLS_PAD, CHANNELS)

    def pick_rows(rows):
        moved = [v[SUBSTEPS, HALO + r].reshape(one) * hot[r].reshape(one) for r in rows]
        chosen = dot(split(jnp.concatenate(moved, axis=0)), pick)
        for n, r in enumerate(rows):
            picked[COLS_PAD * r : COLS_PAD * (r + 1)] = chosen[COLS_PAD * n : COLS_PAD * (n + 1)]

    def uptake_row(r):
        cells = slice(COLS_PAD * r, COLS_PAD * (r + 1))
        p = v[SUBSTEPS, HALO + r].reshape(one)
        halved = halves[r].reshape(one)
        force = drive[cells]
        chosen = picked[cells]
        total = chosen + halved
        inverse = pl.reciprocal(total, approx=True)
        inverse = inverse * (2.0 - total * inverse)
        return cells, p, halved, force, inverse, force * (chosen * inverse)

    def growth_rows(rows, add, spread):
        for n, r in enumerate(rows):
            near = slice(COLS_PAD * n, COLS_PAD * (n + 1))
            cells, p, halved, force, inverse, taken = uptake_row(r)
            if add:
                acc[...] += jnp.sum((taken * p).reshape(ROW), axis=0)
            if spread:
                pull[near] = (rate * force) * p * halved * (inverse * inverse)
                b[0, HALO + r] = (bar0[cells] + rate * taken).reshape(ROW)
        if spread:
            pulled = dot(split(pull[0 : COLS_PAD * len(rows)]), collect)
            for n, r in enumerate(rows):
                part = pulled[COLS_PAD * n : COLS_PAD * (n + 1)]
                b[0, HALO + r] += part.reshape(ROW) * hot[r]

    inner_groups = [range(GROUP * g, GROUP * (g + 1)) for g in range(1, GROUPS - 1)]
    outer = list(range(HALO)) + list(range(ROWS_DEV - HALO, ROWS_DEV))

    for which in (2, 3):
        arrived(0, which)
    unpack_cols(0, v0)
    for step in range(1, SUBSTEPS + 1):
        inner_rows(forward_block, v.at[step], v.at[step - 1], step)
    acc[...] = jnp.zeros_like(acc)

    for rows in inner_groups:
        pick_rows(rows)
        growth_rows(rows, True, False)

    for which in (0, 1, 4, 5, 6, 7):
        arrived(0, which)
    unpack_rows(0, v0)

    halo_rows = list(range(HALO)) + list(range(ALL_ROWS - HALO, ALL_ROWS))
    wide = dot(split(jnp.concatenate([v0[i].reshape(one) for i in halo_rows], axis=0)), spread)
    for n, i in enumerate(halo_rows):
        for k in range(5):
            part = wide[COLS_PAD * n : COLS_PAD * (n + 1), CHANNELS * k : CHANNELS * (k + 1)]
            weights[k, i] = part.reshape(ROW)

    for step in range(1, SUBSTEPS + 1):
        outer_rows(forward_block, weights, v.at[step], v.at[step - 1], step)

    pick_rows(outer)
    growth_rows(outer, True, True)

    def exchange(stage, turn, slot):
        return pltpu.make_async_remote_copy(
            src_ref=gather.at[stage, slot],
            dst_ref=gather.at[stage, slot],
            send_sem=gsend_sem.at[stage, turn],
            recv_sem=grecv_sem.at[stage, slot],
            device_id=peer(stage, turn)[1],
            device_id_type=MESH,
        )

    def stage_start(stage, value):
        gather[stage, places[stage]] = value

        @pl.loop(1, NEAR)
        def _(turn):
            exchange(stage, turn, places[stage]).start()

    def stage_end(stage):
        @pl.loop(1, NEAR)
        def _(turn):
            exchange(stage, turn, peer(stage, turn)[0]).wait_recv()
            exchange(stage, turn, places[stage]).wait_send()

        parts = [gather[stage, n] for n in range(NEAR)]
        while len(parts) > 1:
            parts = [a + c for a, c in zip(parts[0::2], parts[1::2])]
        return parts[0]

    b0 = b.at[0]
    for which in range(4):
        for at, row, column in corner_cells(which, True):
            jj, s = cell(column)
            corner_out[2, which, at : at + 1, :] = b0[HALO + row, jj, s : s + 1, :]
    for which in range(2):
        first = HALO if which == 0 else ROWS_DEV
        for jj in range(BLOCKS):
            cells = [b0[first + r, jj] for r in range(HALO)]
            for n, value in enumerate(pack_bars(cells)):
                row_out[2, which, n, blocked(jj), :] = value
    for which in (0, 1, 4, 5, 6, 7):
        send(2, which)
    stage_start(0, jnp.sum(acc[...], axis=0, keepdims=True))

    for rows in inner_groups:
        growth_rows(rows, False, True)
    b0_cells = b0.reshape(ALL_ROWS * COLS_PAD, CHANNELS)
    for side in range(2):
        cells = []
        for t in range(HALO):
            jj, s = cell(LEFT + t if side == 0 else RIGHT - HALO + t)
            cells.append(b0_cells[column_cells(jj, s), :])
        for n, value in enumerate(pack_bars(cells)):
            col_out[2, side, n] = value
    for which in (2, 3):
        send(2, which)

    def finish(i, jj, total):
        result[i - HALO, blocked(jj), :] = jnp.where(weights[0, i, jj] > 0, total, 0.0)

    goals = [into(b.at[step]) for step in range(1, SUBSTEPS)] + [finish]
    stage_start(1, stage_end(0))
    for which in (2, 3):
        arrived(1, which)
        arrived(2, which)
    unpack_cols(2, b0)
    for step in range(1, SUBSTEPS + 1):
        inner_rows(backward_block, goals[step - 1], b.at[step - 1], step)
    for which in (0, 1):
        arrived(1, which)
    for which in (0, 1, 4, 5, 6, 7):
        arrived(2, which)
    unpack_rows(2, b0)
    for step in range(1, SUBSTEPS + 1):
        outer_rows(backward_block, weights, goals[step - 1], b.at[step - 1], step)
    for phase in range(3):
        for which in range(4 if phase == 1 else 8):
            sent(phase, which)
    totals[...] = stage_end(1)


def finish_kernel(result, totals, out, growth_out, growth, sem):
    count = ROWS_DEV // GROUPS
    copies = [
        pltpu.make_async_copy(
            result.at[pl.ds(count * n, count), pl.ds(LEFT, COLS_DEV), :],
            out.at[pl.ds(count * n, count)],
            sem.at[n],
        )
        for n in range(GROUPS)
    ]
    for copy in copies:
        copy.start()
    lanes = totals[...]
    lanes = (lanes + pltpu.roll(lanes, TRACERS, 1)) * (1.0 / CELLS)
    growth[...] = pltpu.roll(lanes, CHANNELS - FIRST_P, 1)[:, 0:PHYTO]
    copies.append(pltpu.make_async_copy(growth, growth_out, sem.at[GROUPS]))
    copies[GROUPS].start()
    for copy in copies:
        copy.wait()


def shards(
    tracer_state,
    limit_codes,
    center_weight,
    side_weights,
    growth,
    half_sat,
    stoich,
    mortality,
    sinking,
    routing,
    remineral,
    release,
    cotangent,
):
    hbm = pl.BlockSpec(memory_space=pltpu.HBM)
    vmem = pl.BlockSpec(memory_space=pltpu.VMEM)
    padded = (ROWS_DEV, COLS_PAD, CHANNELS)
    cells = (ROWS_DEV,) + ROW
    field = (ALL_ROWS,) + ROW
    halo_rows = (3, 2, 3, COLS_PAD, CHANNELS)
    operands = (
        tracer_state,
        cotangent,
        jnp.transpose(limit_codes, (1, 0, 2)),
        center_weight,
        jnp.transpose(side_weights, (1, 0, 2)),
        growth[None, :],
        mortality[None, :],
        sinking[None, :],
        remineral[None, :],
        half_sat,
        stoich,
        routing,
        release,
    )
    results = pl.pallas_call(
        kernel,
        out_shape=(
            pltpu.VMEM(padded, F32),
            pltpu.VMEM((1, CHANNELS), F32),
        ),
        in_specs=[hbm] * len(operands),
        out_specs=(vmem,) * 2,
        scratch_shapes=[
            pltpu.VMEM(padded, F32),
            pltpu.VMEM(padded, F32),
        ]
        + [pltpu.VMEM(operand.shape, operand.dtype) for operand in operands[2:]]
        + [
            pltpu.VMEM((CHANNELS, CHANNELS), F32),
            pltpu.VMEM((COLS_PAD, CHANNELS), F32),
            pltpu.VMEM((8, CHANNELS), F32),
            pltpu.VMEM((4, CHANNELS, CHANNELS), F32),
            pltpu.VMEM(cells, F32),
            pltpu.VMEM(cells, F32),
            pltpu.VMEM((ROWS_DEV * COLS_PAD, 2 * CHANNELS), BF16),
            pltpu.VMEM((ROWS_DEV * COLS_PAD, 2 * CHANNELS), BF16),
            pltpu.VMEM((ROWS_DEV * COLS_PAD, CHANNELS), F32),
            pltpu.VMEM((ROWS_DEV * COLS_PAD, CHANNELS), F32),
            pltpu.VMEM((ROWS_DEV * COLS_PAD, CHANNELS), F32),
            pltpu.VMEM((ROWS_DEV * COLS_PAD, CHANNELS), F32),
            pltpu.VMEM((5,) + field, F32),
            pltpu.VMEM((SUBSTEPS + 1,) + field, F32),
            pltpu.VMEM((SUBSTEPS,) + field, F32),
            pltpu.VMEM((8, CHANNELS), F32),
            pltpu.VMEM(halo_rows, F32),
            pltpu.VMEM(halo_rows, F32),
            pltpu.VMEM((3, 2, 3, ROWS_DEV, CHANNELS), F32),
            pltpu.VMEM((3, 2, 3, ROWS_DEV, CHANNELS), F32),
            pltpu.VMEM((3, 4, 8, CHANNELS), F32),
            pltpu.VMEM((3, 4, 8, CHANNELS), F32),
            pltpu.VMEM((2, NEAR, 1, CHANNELS), F32),
            pltpu.SemaphoreType.DMA((len(operands),)),
            pltpu.SemaphoreType.DMA((3, 8)),
            pltpu.SemaphoreType.DMA((3, 8)),
            pltpu.SemaphoreType.DMA((2, NEAR)),
            pltpu.SemaphoreType.DMA((2, NEAR)),
        ],
        compiler_params=pltpu.CompilerParams(
            collective_id=0, has_side_effects=True, vmem_limit_bytes=65500000
        ),
        cost_estimate=pl.CostEstimate(flops=10**9, bytes_accessed=3 * 10**6, transcendentals=0),
    )(*operands)
    state_grad, growth_grad = pl.pallas_call(
        finish_kernel,
        out_shape=(
            jax.ShapeDtypeStruct((ROWS_DEV, COLS_DEV, CHANNELS), F32),
            jax.ShapeDtypeStruct((1, PHYTO), F32),
        ),
        in_specs=[vmem] * 2,
        out_specs=(hbm, hbm),
        scratch_shapes=[
            pltpu.VMEM((1, PHYTO), F32),
            pltpu.SemaphoreType.DMA((GROUPS + 1,)),
        ],
        compiler_params=pltpu.CompilerParams(vmem_limit_bytes=32 * 1024 * 1024),
        cost_estimate=pl.CostEstimate(flops=10**8, bytes_accessed=10**6, transcendentals=0),
    )(*results)
    return (state_grad, growth_grad[0])


def solution(mesh):
    in_specs = (
        P("lat", "lon", None),
        P(None, "lat", "lon"),
        P("lat", "lon"),
        P(None, "lat", "lon"),
        P(),
        P(),
        P(),
        P(),
        P(),
        P(),
        P(),
        P(),
        P("lat", "lon", None),
    )
    out_specs = (P("lat", "lon", None), P())
    return jax.shard_map(shards, mesh=mesh, in_specs=in_specs, out_specs=out_specs, check_vma=False)
```

```python
import jax
import jax.numpy as jnp
from jax import lax
from jax.experimental import pallas as pl
from jax.experimental.pallas import tpu as pltpu
from jax.sharding import PartitionSpec as P

TRACERS = 64
PHYTO = 35
NUTRIENTS = 4
ORGANIC = 25
LEVELS = 2
SUBSTEPS = 4
ROWS_DEV = 20
COLS_DEV = 90
CHANNELS = 128
FIRST_P = NUTRIENTS
FIRST_O = NUTRIENTS + PHYTO


HALO = SUBSTEPS
ALL_ROWS = ROWS_DEV + 2 * HALO
BLOCKS = 13
COLS_PAD = 8 * BLOCKS
LEFT = 8
RIGHT = LEFT + COLS_DEV
ROW = (BLOCKS, 8, CHANNELS)
GROUP = 4
GROUPS = ROWS_DEV // GROUP
GROUP_CELLS = GROUP * COLS_PAD
KINDS = 6
CODES = NUTRIENTS + 1
CELLS = 320 * 1440 * LEVELS
MESH = pl.DeviceIdType.MESH
SENT = (3, 1, 3)
MOVES = ((-1, 0), (1, 0), (0, -1), (0, 1), (-1, -1), (-1, 1), (1, -1), (1, 1))
INNER_LOOPS = (0, 3, 2, 2, 2)
RADIX = 4
NEAR = RADIX * RADIX
F32 = jnp.float32
BF16 = jnp.bfloat16


def split(value):
    high = value.astype(BF16)
    low = (value - high.astype(F32)).astype(BF16)
    return jnp.concatenate([high, low], axis=1)


def dot(a, b):
    return jnp.dot(a, b, preferred_element_type=F32)


def cell(column):
    return column % BLOCKS, column // BLOCKS


def blocked(jj):
    return pl.ds(jj, 8, stride=BLOCKS)


def forward_block(weights, dst, src, i, count):
    above = [src[i - 1, jj] for jj in range(BLOCKS)]
    rows = [[src[i + d, jj] for jj in range(BLOCKS)] for d in range(count)]
    under = [src[i + count, jj] for jj in range(BLOCKS)]
    rows = [above] + rows + [under]
    for jj in range(BLOCKS):
        for d in range(count):
            row = rows[d + 1]
            east = row[jj + 1] if jj < BLOCKS - 1 else pltpu.roll(row[0], 7, 0)
            west = row[jj - 1] if jj > 0 else pltpu.roll(row[BLOCKS - 1], 1, 0)
            total = weights[0, i + d, jj] * row[jj]
            total += weights[1, i + d, jj] * east
            total += weights[2, i + d, jj] * west
            total += weights[3, i + d, jj] * rows[d + 2][jj]
            total += weights[4, i + d, jj] * rows[d][jj]
            dst[i + d, jj] = total


def backward_block(weights, put, src, i, count):
    rows = [[src[i + d, jj] for jj in range(BLOCKS)] for d in range(-1, count + 1)]
    for jj in range(BLOCKS):
        for d in range(count):
            row = rows[d + 1]
            if jj > 0:
                from_west = weights[1, i + d, jj - 1] * row[jj - 1]
            else:
                from_west = pltpu.roll(weights[1, i + d, BLOCKS - 1] * row[BLOCKS - 1], 1, 0)
            if jj < BLOCKS - 1:
                from_east = weights[2, i + d, jj + 1] * row[jj + 1]
            else:
                from_east = pltpu.roll(weights[2, i + d, 0] * row[0], 7, 0)
            total = weights[0, i + d, jj] * row[jj]
            total += weights[3, i + d - 1, jj] * rows[d][jj]
            total += weights[4, i + d + 1, jj] * rows[d + 2][jj]
            put(i + d, jj, total + (from_west + from_east))


def outer_rows(block, weights, to, src, step):
    block(weights, to, src, step, HALO)
    block(weights, to, src, ALL_ROWS - HALO - step, HALO)


def into(dst):
    def put(i, jj, total):
        dst[i, jj] = total

    return put


def kernel(
    state_hbm,
    cot_hbm,
    codes_hbm,
    center_hbm,
    sides_hbm,
    growth_hbm,
    mortality_hbm,
    sinking_hbm,
    remineral_hbm,
    half_sat_hbm,
    stoich_hbm,
    routing_hbm,
    release_hbm,
    result,
    totals,
    state,
    cot,
    codes,
    center,
    sides,
    growth,
    mortality,
    sinking,
    remineral,
    half_sat,
    stoich,
    routing,
    release,
    kinds,
    kinds_t,
    vectors,
    pieces,
    hot,
    halves,
    carried,
    parts,
    bar0,
    drive,
    picked,
    pull,
    weights,
    v,
    b,
    acc,
    row_out,
    row_in,
    col_out,
    col_in,
    corner_out,
    corner_in,
    gather,
    load_sem,
    send_sem,
    recv_sem,
    gsend_sem,
    grecv_sem,
):
    lat, lon = lax.axis_index("lat"), lax.axis_index("lon")
    n_lat, n_lon = lax.axis_size("lat"), lax.axis_size("lon")

    def there(move):
        i, j = lat + move[0], lon + move[1]
        return (i >= 0) & (i < n_lat) & (j >= 0) & (j < n_lon)

    def back(move):
        return there((-move[0], -move[1]))

    lat_low, lat_high = lax.rem(lat, RADIX), lax.div(lat, RADIX)
    lon_low, lon_high = lax.rem(lon, RADIX), lax.div(lon, RADIX)
    places = (lat_high * RADIX + lon_high, lat_low * RADIX + lon_low)

    def peer(stage, turn):
        index = lax.rem(places[stage] + turn, NEAR)
        high, low = lax.div(index, RADIX), lax.rem(index, RADIX)
        if stage == 0:
            return index, (high * RADIX + lat_low, low * RADIX + lon_low)
        return index, (lat_high * RADIX + high, lon_high * RADIX + low)

    inner = pl.ds(LEFT, COLS_DEV)
    sources = (
        (codes_hbm, codes),
        (center_hbm, center),
        (sides_hbm, sides),
        (state_hbm, state.at[:, inner, :]),
        (cot_hbm, cot.at[:, inner, :]),
        (growth_hbm, growth),
        (mortality_hbm, mortality),
        (sinking_hbm, sinking),
        (remineral_hbm, remineral),
        (half_sat_hbm, half_sat),
        (stoich_hbm, stoich),
        (routing_hbm, routing),
        (release_hbm, release),
    )
    loads = [
        pltpu.make_async_copy(source, target, load_sem.at[n])
        for n, (source, target) in enumerate(sources)
    ]
    for load in loads:
        load.start()

    barrier = pltpu.get_barrier_semaphore()
    count = jnp.int32(2 * (NEAR - 1))
    for move in MOVES:
        near = there(move)
        count = count + near.astype(jnp.int32)

        @pl.when(near)
        def _():
            pl.semaphore_signal(
                barrier, inc=1, device_id=(lat + move[0], lon + move[1]), device_id_type=MESH
            )

    for stage in range(2):

        @pl.loop(1, NEAR)
        def _(turn):
            pl.semaphore_signal(
                barrier, inc=1, device_id=peer(stage, turn)[1], device_id_type=MESH
            )

    for which, move in enumerate(MOVES):

        @pl.when(jnp.logical_not(back(move)))
        def _():
            for phase in range(3):
                if which < 2:
                    for r in range(SENT[phase]):
                        row_in[phase, which, r, LEFT:RIGHT] = jnp.zeros((COLS_DEV, CHANNELS), F32)
                elif which < 4:
                    col_in[phase, which - 2] = jnp.zeros_like(col_in[phase, which - 2])
                elif phase != 1:
                    corner_in[phase, which - 4] = jnp.zeros_like(corner_in[phase, which - 4])

    left_zeros = jnp.zeros((LEFT, CHANNELS), F32)
    right_zeros = jnp.zeros((COLS_PAD - RIGHT, CHANNELS), F32)

    @pl.loop(0, ROWS_DEV)
    def _(i):
        state[i, 0:LEFT] = left_zeros
        state[i, RIGHT:COLS_PAD] = right_zeros
        cot[i, 0:LEFT] = left_zeros
        cot[i, RIGHT:COLS_PAD] = right_zeros

    for phase in range(3):
        for which in range(2):
            for r in range(SENT[phase]):
                row_in[phase, which, r, 0:LEFT] = left_zeros
                row_in[phase, which, r, RIGHT:COLS_PAD] = right_zeros
    corner_out[...] = jnp.zeros_like(corner_out)

    kinds[...] = jnp.zeros_like(kinds)
    kinds_t[...] = jnp.zeros_like(kinds_t)
    for load in loads[:3]:
        load.wait()
    upper_code, lower_code = codes[:, 0, :], codes[:, 1, :]
    wet = (upper_code != NUTRIENTS).astype(F32)
    every = lambda k: pl.ds(k, ROWS_DEV, stride=KINDS)
    kinds[every(0), 0:COLS_DEV] = wet * center[...]
    for s in range(4):
        kinds[every(s + 1), 0:COLS_DEV] = wet * sides[:, s, :]
    kinds[every(5), 0:COLS_DEV] = (upper_code + CODES * lower_code).astype(F32)
    kinds_t[LEFT:RIGHT] = kinds[...].T[0:COLS_DEV]

    lane = lax.broadcasted_iota(jnp.int32, (1, CHANNELS), 1)
    lane_in = lax.rem(lane, TRACERS)
    organic = lane_in >= FIRST_O
    loads[3].wait()

    def carry(i, low, high):
        turned = pltpu.roll(kinds_t[low:high], (FIRST_O - KINDS * i) % CHANNELS, 1)
        wide = jnp.broadcast_to(turned[:, FIRST_O : FIRST_O + 1], (high - low, CHANNELS))
        masked = jnp.where(wide > 0, state[i, low:high], 0.0)
        state[i, low:high] = jnp.where(organic, turned, masked)

    for i in range(ROWS_DEV):
        if i < HALO or i >= ROWS_DEV - HALO:
            carry(i, 0, COLS_PAD)
        else:
            carry(i, LEFT, LEFT + 8)
            carry(i, 88, COLS_PAD)

    lane_free = lane_in >= FIRST_O + 5

    def turn_by(value, shift):
        return pltpu.roll(value, shift % CHANNELS, 1)

    def pack_state(cells):
        return [
            jnp.where(lane_free, turn_by(cells[3], FIRST_O + 5 - 20 * n), cells[n]) for n in range(3)
        ]

    def unpack_state(sent_cells):
        last = [turn_by(sent_cells[n], 20 * n - FIRST_O - 5) for n in range(3)]
        last = jnp.where(lane_in < 20, last[0], jnp.where(lane_in < 40, last[1], last[2]))
        return list(sent_cells) + [last]

    first_part = FIRST_O + TRACERS - 2 * ORGANIC

    def pack_organic(cells):
        others = jnp.where(
            lane_in >= first_part - FIRST_O,
            turn_by(cells[1], -ORGANIC),
            turn_by(cells[2], -FIRST_O),
        )
        return [jnp.where(organic, cells[0], others)]

    def pack_bars(cells):
        second = jnp.where(organic, turn_by(cells[3], FIRST_O - ORGANIC), cells[1])
        return [
            jnp.where(organic, turn_by(cells[3], FIRST_O), cells[0]),
            jnp.where(lane_in >= first_part, cells[2], second),
            jnp.where(organic, cells[3], cells[2]),
        ]

    def unpack_bars(sent_cells, early):
        third = jnp.where(organic, turn_by(early, FIRST_O), sent_cells[2])
        last = jnp.where(
            lane_in < ORGANIC,
            turn_by(sent_cells[0], -FIRST_O),
            turn_by(sent_cells[1], ORGANIC - FIRST_O),
        )
        return [
            jnp.where(organic, early, sent_cells[0]),
            jnp.where(organic, turn_by(early, ORGANIC), sent_cells[1]),
            jnp.where(lane_in >= first_part, sent_cells[1], third),
            jnp.where(organic, sent_cells[2], last),
        ]

    def received_cols(phase, side):
        cells = [col_in[phase, side, n] for n in range(3)]
        if phase == 0:
            return unpack_state(cells)
        return unpack_bars(cells, col_in[1, side, 0])

    def received_rows(phase, which, jj):
        cells = [row_in[phase, which, n, blocked(jj), :] for n in range(3)]
        if phase == 0:
            return unpack_state(cells)
        return unpack_bars(cells, row_in[1, which, 0, blocked(jj), :])

    def message(phase, which):
        move = MOVES[which]
        sent_rows = pl.ds(0, SENT[phase])
        if which < 2:
            source = row_out.at[phase, which, sent_rows, inner, :]
            target = row_in.at[phase, which, sent_rows, inner, :]
        elif which < 4:
            source = col_out.at[phase, which - 2, sent_rows]
            target = col_in.at[phase, which - 2, sent_rows]
        else:
            source, target = corner_out.at[phase, which - 4], corner_in.at[phase, which - 4]
        return pltpu.make_async_remote_copy(
            src_ref=source,
            dst_ref=target,
            send_sem=send_sem.at[phase, which],
            recv_sem=recv_sem.at[phase, which],
            device_id=(lat + move[0], lon + move[1]),
            device_id_type=MESH,
        )

    def send(phase, which):
        @pl.when(there(MOVES[which]))
        def _():
            message(phase, which).start()

    def sent(phase, which):
        @pl.when(there(MOVES[which]))
        def _():
            message(phase, which).wait_send()

    def arrived(phase, which):
        @pl.when(back(MOVES[which]))
        def _():
            message(phase, which).wait_recv()

    def corner_cells(which, inside):
        down, right = MOVES[4 + which]
        at = 0
        for depth in range(3):
            for t in range(3 - depth):
                if inside:
                    row = depth if down < 0 else ROWS_DEV - 1 - depth
                    column = LEFT + t if right < 0 else RIGHT - 1 - t
                else:
                    row = ROWS_DEV + depth if down < 0 else -1 - depth
                    column = RIGHT + t if right < 0 else LEFT - 1 - t
                yield at, row, column
                at += 1

    weight_cells = weights.reshape(5 * ALL_ROWS * COLS_PAD, CHANNELS)

    def column_cells(jj, s, base=0):
        return pl.ds(base + HALO * COLS_PAD + 8 * jj + s, ROWS_DEV, stride=COLS_PAD)

    def unpack_cols(phase, field):
        cells = field.reshape(ALL_ROWS * COLS_PAD, CHANNELS)
        for side in range(2):
            halo = received_cols(phase, side)
            for t in range(HALO):
                jj, s = cell(RIGHT + t if side == 0 else LEFT - HALO + t)
                cells[column_cells(jj, s), :] = halo[t]
                for k in range(5 if phase == 0 else 0):
                    weight_cells[column_cells(jj, s, k * ALL_ROWS * COLS_PAD), :] = (
                        jnp.broadcast_to(
                            halo[t][:, FIRST_O + k : FIRST_O + k + 1], (ROWS_DEV, CHANNELS)
                        )
                    )

    def unpack_rows(phase, field):
        for which in range(2):
            first = ALL_ROWS - HALO if which == 0 else 0
            for jj in range(BLOCKS):
                for r, cells in enumerate(received_rows(phase, which, jj)):
                    field[first + r, jj] = cells

        for which in range(4):
            for at, row, column in corner_cells(which, False):
                jj, s = cell(column)
                field[HALO + row, jj, s : s + 1, :] = corner_in[phase, which, at : at + 1, :]

    state_cells = state.reshape(ROWS_DEV * COLS_PAD, CHANNELS)
    for side in range(2):
        at = LEFT if side == 0 else RIGHT - HALO
        cells = [state_cells[pl.ds(at + t, ROWS_DEV, stride=COLS_PAD), :] for t in range(HALO)]
        for n, value in enumerate(pack_state(cells)):
            col_out[0, side, n] = value
    for which in range(2):
        first = 0 if which == 0 else ROWS_DEV - HALO
        for n, value in enumerate(pack_state([state[first + r] for r in range(HALO)])):
            row_out[0, which, n] = value

    for which in range(4):
        for at, row, column in corner_cells(which, True):
            corner_out[0, which, at : at + 1] = state[row, column : column + 1]

    order = (2, 3, 0, 1, 4, 5, 6, 7)
    pl.semaphore_wait(barrier, count)
    for which in order:
        send(0, which)

    v0 = v.at[0]

    lane_f = lane_in.astype(F32)
    upper = lane < TRACERS

    for load in loads[5:]:
        load.wait()
    vectors[...] = jnp.zeros_like(vectors)
    pieces[...] = jnp.zeros_like(pieces)
    for l in range(LEVELS):
        n, p, o = l * TRACERS, l * TRACERS + FIRST_P, l * TRACERS + FIRST_O
        end = (l + 1) * TRACERS
        vectors[0:1, p:o] = growth[...]
        vectors[1:2, p:o] = mortality[...]
        vectors[2:3, p:o] = sinking[...]
        vectors[3:4, o:end] = remineral[...]
        pieces[0, n : n + NUTRIENTS, p:o] = stoich[...]
        pieces[1, o:end, p:o] = routing[...]
        pieces[2, n : n + NUTRIENTS, o:end] = release[...]
        pieces[3, n : n + NUTRIENTS, p:o] = half_sat[...]
    rate, lost, sunk, decayed = (vectors[n : n + 1, :] for n in range(4))

    row_lane = lax.broadcasted_iota(jnp.int32, (CHANNELS, CHANNELS), 0)
    col_lane = lax.broadcasted_iota(jnp.int32, (CHANNELS, CHANNELS), 1)
    same = (row_lane < TRACERS) == (col_lane < TRACERS)
    row_in_level = lax.rem(row_lane, TRACERS)
    col_in_level = lax.rem(col_lane, TRACERS)
    row_p = (row_in_level >= FIRST_P) & (row_in_level < FIRST_O)
    col_p = (col_in_level >= FIRST_P) & (col_in_level < FIRST_O)
    own = jnp.where(row_lane == col_lane, 1.0, 0.0)
    own_p = jnp.where((row_lane == col_lane) & col_p, 1.0, 0.0)
    below = jnp.where(row_lane == col_lane + TRACERS, 1.0, 0.0)
    bars = own * ((1.0 - lost) * (1.0 - sunk) * (1.0 - decayed))
    bars += below * ((1.0 - lost) * sunk) + pieces[1] * lost + pieces[2] * decayed
    light = jnp.where(upper, 1.0, 0.4)
    drives = light * (own_p * (1.0 - sunk) + below * sunk - pieces[0])
    ones = jnp.where(col_p[0:1], 0.0, 1.0)
    halves_of = [pieces[3, k : k + 1, :] + pieces[3, TRACERS + k : TRACERS + k + 1, :] + ones for k in range(NUTRIENTS)]
    pick = jnp.where(same & (row_in_level < NUTRIENTS) & col_p, 1.0, 0.0).astype(BF16)
    collect = jnp.where(same & (col_in_level < NUTRIENTS) & row_p, 1.0, 0.0).astype(BF16)
    pick = jnp.concatenate([pick, pick], axis=0)
    collect = jnp.concatenate([collect, collect], axis=0)
    maps = jnp.concatenate([bars, drives], axis=1)
    maps_high = maps.astype(BF16)
    maps_low = (maps - maps_high.astype(F32)).astype(BF16)
    maps_twice = jnp.concatenate([maps_high, maps_high], axis=0)

    for i in range(HALO, ROWS_DEV - HALO):
        turned = pltpu.roll(kinds_t[16:88], (FIRST_O - KINDS * i) % CHANNELS, 1)
        state[i, 16:88] = jnp.where(organic, turned, state[i, 16:88])
    spread = jnp.concatenate(
        [jnp.where(row_lane == FIRST_O + k, 1.0, 0.0).astype(BF16) for k in range(5)], axis=1
    )
    spread = jnp.concatenate([spread, spread], axis=0)
    for n in range(ROWS_DEV // 2):
        block = jnp.concatenate(
            [state[2 * n + r, blocked(jj), :] for r in range(2) for jj in range(BLOCKS)], axis=0
        )
        carried[2 * COLS_PAD * n : 2 * COLS_PAD * (n + 1)] = split(block)
    for g in range(GROUPS):
        cells = pl.ds(GROUP_CELLS * g, GROUP_CELLS)
        wide = dot(carried[cells], spread)
        for k in range(5):
            part = wide[:, CHANNELS * k : CHANNELS * (k + 1)]
            weights[k, HALO + GROUP * g : HALO + GROUP * (g + 1)] = part.reshape((GROUP,) + ROW)
        for i in range(GROUP * g, GROUP * (g + 1)):
            for jj in range(BLOCKS):
                cells = state[i, blocked(jj), :]
                v0[HALO + i, jj] = jnp.where(weights[0, HALO + i, jj] > 0, cells, 0.0)
                code = jnp.broadcast_to(cells[:, FIRST_O + 5 : FIRST_O + 6], (8, CHANNELS))
                second = jnp.floor((code + 0.5) * (1.0 / CODES))
                here = jnp.where(upper, code - CODES * second, second)
                hot[i, jj] = jnp.where(here == lane_f, 1.0, 0.0)
                halved = jnp.ones((8, CHANNELS), F32)
                for k in range(NUTRIENTS):
                    halved = jnp.where(here == k, halves_of[k], halved)
                halves[i, jj] = halved

    loads[4].wait()
    for n in range(ROWS_DEV // 2):
        block = jnp.concatenate(
            [cot[2 * n + r, blocked(jj), :] for r in range(2) for jj in range(BLOCKS)], axis=0
        )
        parts[2 * COLS_PAD * n : 2 * COLS_PAD * (n + 1)] = split(block)
    for n in range(GROUPS):
        cells = pl.ds(GROUP_CELLS * n, GROUP_CELLS)
        both = dot(parts[cells], maps_twice) + dot(parts[cells, 0:CHANNELS], maps_low)
        bar0[cells] = both[:, :CHANNELS]
        drive[cells] = both[:, CHANNELS:]

    for side in range(2):
        cells = []
        for t in range(HALO):
            jj, s = cell(LEFT + t if side == 0 else RIGHT - HALO + t)
            cells.append(bar0[pl.ds(8 * jj + s, ROWS_DEV, stride=COLS_PAD), :])
        for n, value in enumerate(pack_organic(cells)):
            col_out[1, side, n] = value
    for which in range(2):
        first = 0 if which == 0 else ROWS_DEV - HALO
        for jj in range(BLOCKS):
            cells = [
                bar0[COLS_PAD * (first + r) + 8 * jj : COLS_PAD * (first + r) + 8 * jj + 8]
                for r in range(HALO)
            ]
            for n, value in enumerate(pack_organic(cells)):
                row_out[1, which, n, blocked(jj), :] = value
    for which in range(4):
        send(1, which)

    def inner_rows(block, to, src, step):
        count = (ROWS_DEV - 2 * step) // INNER_LOOPS[step]

        @pl.loop(0, INNER_LOOPS[step])
        def _(n):
            block(weights, to, src, HALO + step + count * n, count)

    one = (COLS_PAD, CHANNELS)

    def pick_rows(rows):
        moved = [v[SUBSTEPS, HALO + r].reshape(one) * hot[r].reshape(one) for r in rows]
        chosen = dot(split(jnp.concatenate(moved, axis=0)), pick)
        for n, r in enumerate(rows):
            picked[COLS_PAD * r : COLS_PAD * (r + 1)] = chosen[COLS_PAD * n : COLS_PAD * (n + 1)]

    def uptake_row(r):
        cells = slice(COLS_PAD * r, COLS_PAD * (r + 1))
        p = v[SUBSTEPS, HALO + r].reshape(one)
        halved = halves[r].reshape(one)
        force = drive[cells]
        chosen = picked[cells]
        total = chosen + halved
        inverse = pl.reciprocal(total, approx=True)
        inverse = inverse * (2.0 - total * inverse)
        return cells, p, halved, force, inverse, force * (chosen * inverse)

    def growth_rows(rows, add, spread):
        for n, r in enumerate(rows):
            near = slice(COLS_PAD * n, COLS_PAD * (n + 1))
            cells, p, halved, force, inverse, taken = uptake_row(r)
            if add:
                acc[...] += jnp.sum((taken * p).reshape(ROW), axis=0)
            if spread:
                pull[near] = (rate * force) * p * halved * (inverse * inverse)
                b[0, HALO + r] = (bar0[cells] + rate * taken).reshape(ROW)
        if spread:
            pulled = dot(split(pull[0 : COLS_PAD * len(rows)]), collect)
            for n, r in enumerate(rows):
                part = pulled[COLS_PAD * n : COLS_PAD * (n + 1)]
                b[0, HALO + r] += part.reshape(ROW) * hot[r]

    inner_groups = [range(GROUP * g, GROUP * (g + 1)) for g in range(1, GROUPS - 1)]
    outer = list(range(HALO)) + list(range(ROWS_DEV - HALO, ROWS_DEV))

    for which in (2, 3):
        arrived(0, which)
    unpack_cols(0, v0)
    for step in range(1, SUBSTEPS + 1):
        inner_rows(forward_block, v.at[step], v.at[step - 1], step)
    acc[...] = jnp.zeros_like(acc)

    for rows in inner_groups:
        pick_rows(rows)
        growth_rows(rows, True, False)

    for which in (0, 1, 4, 5, 6, 7):
        arrived(0, which)
    unpack_rows(0, v0)

    halo_rows = list(range(HALO)) + list(range(ALL_ROWS - HALO, ALL_ROWS))
    wide = dot(split(jnp.concatenate([v0[i].reshape(one) for i in halo_rows], axis=0)), spread)
    for n, i in enumerate(halo_rows):
        for k in range(5):
            part = wide[COLS_PAD * n : COLS_PAD * (n + 1), CHANNELS * k : CHANNELS * (k + 1)]
            weights[k, i] = part.reshape(ROW)

    for step in range(1, SUBSTEPS + 1):
        outer_rows(forward_block, weights, v.at[step], v.at[step - 1], step)

    pick_rows(outer)
    growth_rows(outer, True, True)

    def exchange(stage, turn, slot):
        return pltpu.make_async_remote_copy(
            src_ref=gather.at[stage, slot],
            dst_ref=gather.at[stage, slot],
            send_sem=gsend_sem.at[stage, turn],
            recv_sem=grecv_sem.at[stage, slot],
            device_id=peer(stage, turn)[1],
            device_id_type=MESH,
        )

    def stage_start(stage, value):
        gather[stage, places[stage]] = value

        @pl.loop(1, NEAR)
        def _(turn):
            exchange(stage, turn, places[stage]).start()

    def stage_end(stage):
        @pl.loop(1, NEAR)
        def _(turn):
            exchange(stage, turn, peer(stage, turn)[0]).wait_recv()
            exchange(stage, turn, places[stage]).wait_send()

        parts = [gather[stage, n] for n in range(NEAR)]
        while len(parts) > 1:
            parts = [a + c for a, c in zip(parts[0::2], parts[1::2])]
        return parts[0]

    stage_start(0, jnp.sum(acc[...], axis=0, keepdims=True))
    b0 = b.at[0]
    for which in range(4):
        for at, row, column in corner_cells(which, True):
            jj, s = cell(column)
            corner_out[2, which, at : at + 1, :] = b0[HALO + row, jj, s : s + 1, :]
    for which in range(2):
        first = HALO if which == 0 else ROWS_DEV
        for jj in range(BLOCKS):
            cells = [b0[first + r, jj] for r in range(HALO)]
            for n, value in enumerate(pack_bars(cells)):
                row_out[2, which, n, blocked(jj), :] = value
    for which in (0, 1, 4, 5, 6, 7):
        send(2, which)

    for rows in inner_groups:
        growth_rows(rows, False, True)
    b0_cells = b0.reshape(ALL_ROWS * COLS_PAD, CHANNELS)
    for side in range(2):
        cells = []
        for t in range(HALO):
            jj, s = cell(LEFT + t if side == 0 else RIGHT - HALO + t)
            cells.append(b0_cells[column_cells(jj, s), :])
        for n, value in enumerate(pack_bars(cells)):
            col_out[2, side, n] = value
    for which in (2, 3):
        send(2, which)

    def finish(i, jj, total):
        result[i - HALO, blocked(jj), :] = jnp.where(weights[0, i, jj] > 0, total, 0.0)

    goals = [into(b.at[step]) for step in range(1, SUBSTEPS)] + [finish]
    stage_start(1, stage_end(0))
    for which in (2, 3):
        arrived(1, which)
        arrived(2, which)
    unpack_cols(2, b0)
    for step in range(1, SUBSTEPS + 1):
        inner_rows(backward_block, goals[step - 1], b.at[step - 1], step)
    for which in (0, 1):
        arrived(1, which)
    for which in (0, 1, 4, 5, 6, 7):
        arrived(2, which)
    unpack_rows(2, b0)
    for step in range(1, SUBSTEPS + 1):
        outer_rows(backward_block, weights, goals[step - 1], b.at[step - 1], step)
    for phase in range(3):
        for which in range(4 if phase == 1 else 8):
            sent(phase, which)
    totals[...] = stage_end(1)


def finish_kernel(result, totals, out, growth_out, growth, sem):
    count = ROWS_DEV // GROUPS
    copies = [
        pltpu.make_async_copy(
            result.at[pl.ds(count * n, count), pl.ds(LEFT, COLS_DEV), :],
            out.at[pl.ds(count * n, count)],
            sem.at[n],
        )
        for n in range(GROUPS)
    ]
    for copy in copies:
        copy.start()
    lanes = totals[...]
    lanes = (lanes + pltpu.roll(lanes, TRACERS, 1)) * (1.0 / CELLS)
    growth[...] = pltpu.roll(lanes, CHANNELS - FIRST_P, 1)[:, 0:PHYTO]
    copies.append(pltpu.make_async_copy(growth, growth_out, sem.at[GROUPS]))
    copies[GROUPS].start()
    for copy in copies:
        copy.wait()


def shards(
    tracer_state,
    limit_codes,
    center_weight,
    side_weights,
    growth,
    half_sat,
    stoich,
    mortality,
    sinking,
    routing,
    remineral,
    release,
    cotangent,
):
    hbm = pl.BlockSpec(memory_space=pltpu.HBM)
    vmem = pl.BlockSpec(memory_space=pltpu.VMEM)
    padded = (ROWS_DEV, COLS_PAD, CHANNELS)
    cells = (ROWS_DEV,) + ROW
    field = (ALL_ROWS,) + ROW
    halo_rows = (3, 2, 3, COLS_PAD, CHANNELS)
    operands = (
        tracer_state,
        cotangent,
        jnp.transpose(limit_codes, (1, 0, 2)),
        center_weight,
        jnp.transpose(side_weights, (1, 0, 2)),
        growth[None, :],
        mortality[None, :],
        sinking[None, :],
        remineral[None, :],
        half_sat,
        stoich,
        routing,
        release,
    )
    results = pl.pallas_call(
        kernel,
        out_shape=(
            pltpu.VMEM(padded, F32),
            pltpu.VMEM((1, CHANNELS), F32),
        ),
        in_specs=[hbm] * len(operands),
        out_specs=(vmem,) * 2,
        scratch_shapes=[
            pltpu.VMEM(padded, F32),
            pltpu.VMEM(padded, F32),
        ]
        + [pltpu.VMEM(operand.shape, operand.dtype) for operand in operands[2:]]
        + [
            pltpu.VMEM((CHANNELS, CHANNELS), F32),
            pltpu.VMEM((COLS_PAD, CHANNELS), F32),
            pltpu.VMEM((8, CHANNELS), F32),
            pltpu.VMEM((4, CHANNELS, CHANNELS), F32),
            pltpu.VMEM(cells, F32),
            pltpu.VMEM(cells, F32),
            pltpu.VMEM((ROWS_DEV * COLS_PAD, 2 * CHANNELS), BF16),
            pltpu.VMEM((ROWS_DEV * COLS_PAD, 2 * CHANNELS), BF16),
            pltpu.VMEM((ROWS_DEV * COLS_PAD, CHANNELS), F32),
            pltpu.VMEM((ROWS_DEV * COLS_PAD, CHANNELS), F32),
            pltpu.VMEM((ROWS_DEV * COLS_PAD, CHANNELS), F32),
            pltpu.VMEM((ROWS_DEV * COLS_PAD, CHANNELS), F32),
            pltpu.VMEM((5,) + field, F32),
            pltpu.VMEM((SUBSTEPS + 1,) + field, F32),
            pltpu.VMEM((SUBSTEPS,) + field, F32),
            pltpu.VMEM((8, CHANNELS), F32),
            pltpu.VMEM(halo_rows, F32),
            pltpu.VMEM(halo_rows, F32),
            pltpu.VMEM((3, 2, 3, ROWS_DEV, CHANNELS), F32),
            pltpu.VMEM((3, 2, 3, ROWS_DEV, CHANNELS), F32),
            pltpu.VMEM((3, 4, 8, CHANNELS), F32),
            pltpu.VMEM((3, 4, 8, CHANNELS), F32),
            pltpu.VMEM((2, NEAR, 1, CHANNELS), F32),
            pltpu.SemaphoreType.DMA((len(operands),)),
            pltpu.SemaphoreType.DMA((3, 8)),
            pltpu.SemaphoreType.DMA((3, 8)),
            pltpu.SemaphoreType.DMA((2, NEAR)),
            pltpu.SemaphoreType.DMA((2, NEAR)),
        ],
        compiler_params=pltpu.CompilerParams(
            collective_id=0, has_side_effects=True, vmem_limit_bytes=65500000
        ),
        cost_estimate=pl.CostEstimate(flops=10**9, bytes_accessed=3 * 10**6, transcendentals=0),
    )(*operands)
    state_grad, growth_grad = pl.pallas_call(
        finish_kernel,
        out_shape=(
            jax.ShapeDtypeStruct((ROWS_DEV, COLS_DEV, CHANNELS), F32),
            jax.ShapeDtypeStruct((1, PHYTO), F32),
        ),
        in_specs=[vmem] * 2,
        out_specs=(hbm, hbm),
        scratch_shapes=[
            pltpu.VMEM((1, PHYTO), F32),
            pltpu.SemaphoreType.DMA((GROUPS + 1,)),
        ],
        compiler_params=pltpu.CompilerParams(vmem_limit_bytes=32 * 1024 * 1024),
        cost_estimate=pl.CostEstimate(flops=10**8, bytes_accessed=10**6, transcendentals=0),
    )(*results)
    return (state_grad, growth_grad[0])


def solution(mesh):
    in_specs = (
        P("lat", "lon", None),
        P(None, "lat", "lon"),
        P("lat", "lon"),
        P(None, "lat", "lon"),
        P(),
        P(),
        P(),
        P(),
        P(),
        P(),
        P(),
        P(),
        P("lat", "lon", None),
    )
    out_specs = (P("lat", "lon", None), P())
    return jax.shard_map(shards, mesh=mesh, in_specs=in_specs, out_specs=out_specs, check_vma=False)
```

```python
import jax
import jax.numpy as jnp
from jax import lax
from jax.experimental import pallas as pl
from jax.experimental.pallas import tpu as pltpu
from jax.sharding import PartitionSpec as P

TRACERS = 64
PHYTO = 35
NUTRIENTS = 4
ORGANIC = 25
LEVELS = 2
SUBSTEPS = 4
ROWS_DEV = 20
COLS_DEV = 90
CHANNELS = 128
FIRST_P = NUTRIENTS
FIRST_O = NUTRIENTS + PHYTO


HALO = SUBSTEPS
ALL_ROWS = ROWS_DEV + 2 * HALO
BLOCKS = 13
COLS_PAD = 8 * BLOCKS
LEFT = 8
RIGHT = LEFT + COLS_DEV
ROW = (BLOCKS, 8, CHANNELS)
GROUP = 4
GROUPS = ROWS_DEV // GROUP
GROUP_CELLS = GROUP * COLS_PAD
KINDS = 6
CODES = NUTRIENTS + 1
CELLS = 320 * 1440 * LEVELS
MESH = pl.DeviceIdType.MESH
SENT = (3, 1, 3)
MOVES = ((-1, 0), (1, 0), (0, -1), (0, 1), (-1, -1), (-1, 1), (1, -1), (1, 1))
INNER_LOOPS = (0, 3, 2, 2, 2)
RADIX = 4
NEAR = RADIX * RADIX
F32 = jnp.float32
BF16 = jnp.bfloat16


def split(value):
    high = value.astype(BF16)
    low = (value - high.astype(F32)).astype(BF16)
    return jnp.concatenate([high, low], axis=1)


def dot(a, b):
    return jnp.dot(a, b, preferred_element_type=F32)


def cell(column):
    return column % BLOCKS, column // BLOCKS


def blocked(jj):
    return pl.ds(jj, 8, stride=BLOCKS)


def forward_block(weights, dst, src, i, count):
    above = [src[i - 1, jj] for jj in range(BLOCKS)]
    rows = [[src[i + d, jj] for jj in range(BLOCKS)] for d in range(count)]
    under = [src[i + count, jj] for jj in range(BLOCKS)]
    rows = [above] + rows + [under]
    for jj in range(BLOCKS):
        for d in range(count):
            row = rows[d + 1]
            east = row[jj + 1] if jj < BLOCKS - 1 else pltpu.roll(row[0], 7, 0)
            west = row[jj - 1] if jj > 0 else pltpu.roll(row[BLOCKS - 1], 1, 0)
            total = weights[0, i + d, jj] * row[jj]
            total += weights[1, i + d, jj] * east
            total += weights[2, i + d, jj] * west
            total += weights[3, i + d, jj] * rows[d + 2][jj]
            total += weights[4, i + d, jj] * rows[d][jj]
            dst[i + d, jj] = total


def backward_block(weights, put, src, i, count):
    rows = [[src[i + d, jj] for jj in range(BLOCKS)] for d in range(-1, count + 1)]
    for jj in range(BLOCKS):
        for d in range(count):
            row = rows[d + 1]
            if jj > 0:
                from_west = weights[1, i + d, jj - 1] * row[jj - 1]
            else:
                from_west = pltpu.roll(weights[1, i + d, BLOCKS - 1] * row[BLOCKS - 1], 1, 0)
            if jj < BLOCKS - 1:
                from_east = weights[2, i + d, jj + 1] * row[jj + 1]
            else:
                from_east = pltpu.roll(weights[2, i + d, 0] * row[0], 7, 0)
            total = weights[0, i + d, jj] * row[jj]
            total += weights[3, i + d - 1, jj] * rows[d][jj]
            total += weights[4, i + d + 1, jj] * rows[d + 2][jj]
            put(i + d, jj, total + (from_west + from_east))


def outer_rows(block, weights, to, src, step):
    block(weights, to, src, step, HALO)
    block(weights, to, src, ALL_ROWS - HALO - step, HALO)


def into(dst):
    def put(i, jj, total):
        dst[i, jj] = total

    return put


def kernel(
    state_hbm,
    cot_hbm,
    codes_hbm,
    center_hbm,
    sides_hbm,
    growth_hbm,
    mortality_hbm,
    sinking_hbm,
    remineral_hbm,
    half_sat_hbm,
    stoich_hbm,
    routing_hbm,
    release_hbm,
    result,
    totals,
    state,
    cot,
    codes,
    center,
    sides,
    growth,
    mortality,
    sinking,
    remineral,
    half_sat,
    stoich,
    routing,
    release,
    kinds,
    kinds_t,
    vectors,
    pieces,
    hot,
    halves,
    bar0,
    drive,
    picked,
    pull,
    weights,
    v,
    b,
    acc,
    row_out,
    row_in,
    col_out,
    col_in,
    corner_out,
    corner_in,
    gather,
    load_sem,
    send_sem,
    recv_sem,
    gsend_sem,
    grecv_sem,
):
    lat, lon = lax.axis_index("lat"), lax.axis_index("lon")
    n_lat, n_lon = lax.axis_size("lat"), lax.axis_size("lon")

    def there(move):
        i, j = lat + move[0], lon + move[1]
        return (i >= 0) & (i < n_lat) & (j >= 0) & (j < n_lon)

    def back(move):
        return there((-move[0], -move[1]))

    lat_low, lat_high = lax.rem(lat, RADIX), lax.div(lat, RADIX)
    lon_low, lon_high = lax.rem(lon, RADIX), lax.div(lon, RADIX)
    places = (lat_high * RADIX + lon_high, lat_low * RADIX + lon_low)

    def peer(stage, turn):
        index = lax.rem(places[stage] + turn, NEAR)
        high, low = lax.div(index, RADIX), lax.rem(index, RADIX)
        if stage == 0:
            return index, (high * RADIX + lat_low, low * RADIX + lon_low)
        return index, (lat_high * RADIX + high, lon_high * RADIX + low)

    inner = pl.ds(LEFT, COLS_DEV)
    sources = (
        (codes_hbm, codes),
        (center_hbm, center),
        (sides_hbm, sides),
        (state_hbm, state.at[:, inner, :]),
        (cot_hbm, cot.at[:, inner, :]),
        (growth_hbm, growth),
        (mortality_hbm, mortality),
        (sinking_hbm, sinking),
        (remineral_hbm, remineral),
        (half_sat_hbm, half_sat),
        (stoich_hbm, stoich),
        (routing_hbm, routing),
        (release_hbm, release),
    )
    loads = [
        pltpu.make_async_copy(source, target, load_sem.at[n])
        for n, (source, target) in enumerate(sources)
    ]
    for load in loads:
        load.start()

    barrier = pltpu.get_barrier_semaphore()
    count = jnp.int32(2 * (NEAR - 1))
    for move in MOVES:
        near = there(move)
        count = count + near.astype(jnp.int32)

        @pl.when(near)
        def _():
            pl.semaphore_signal(
                barrier, inc=1, device_id=(lat + move[0], lon + move[1]), device_id_type=MESH
            )

    for stage in range(2):

        @pl.loop(1, NEAR)
        def _(turn):
            pl.semaphore_signal(
                barrier, inc=1, device_id=peer(stage, turn)[1], device_id_type=MESH
            )

    for which, move in enumerate(MOVES):

        @pl.when(jnp.logical_not(back(move)))
        def _():
            for phase in range(3):
                if which < 2:
                    for r in range(SENT[phase]):
                        row_in[phase, which, r, LEFT:RIGHT] = jnp.zeros((COLS_DEV, CHANNELS), F32)
                elif which < 4:
                    col_in[phase, which - 2] = jnp.zeros_like(col_in[phase, which - 2])
                elif phase != 1:
                    corner_in[phase, which - 4] = jnp.zeros_like(corner_in[phase, which - 4])

    left_zeros = jnp.zeros((LEFT, CHANNELS), F32)
    right_zeros = jnp.zeros((COLS_PAD - RIGHT, CHANNELS), F32)

    @pl.loop(0, ROWS_DEV)
    def _(i):
        state[i, 0:LEFT] = left_zeros
        state[i, RIGHT:COLS_PAD] = right_zeros
        cot[i, 0:LEFT] = left_zeros
        cot[i, RIGHT:COLS_PAD] = right_zeros

    for phase in range(3):
        for which in range(2):
            for r in range(SENT[phase]):
                row_in[phase, which, r, 0:LEFT] = left_zeros
                row_in[phase, which, r, RIGHT:COLS_PAD] = right_zeros
    corner_out[...] = jnp.zeros_like(corner_out)

    kinds[...] = jnp.zeros_like(kinds)
    kinds_t[...] = jnp.zeros_like(kinds_t)
    for load in loads[:3]:
        load.wait()
    upper_code, lower_code = codes[:, 0, :], codes[:, 1, :]
    wet = (upper_code != NUTRIENTS).astype(F32)
    every = lambda k: pl.ds(k, ROWS_DEV, stride=KINDS)
    kinds[every(0), 0:COLS_DEV] = wet * center[...]
    for s in range(4):
        kinds[every(s + 1), 0:COLS_DEV] = wet * sides[:, s, :]
    kinds[every(5), 0:COLS_DEV] = (upper_code + CODES * lower_code).astype(F32)
    kinds_t[LEFT:RIGHT] = kinds[...].T[0:COLS_DEV]

    lane = lax.broadcasted_iota(jnp.int32, (1, CHANNELS), 1)
    lane_in = lax.rem(lane, TRACERS)
    organic = lane_in >= FIRST_O
    loads[3].wait()

    def carry(i, low, high):
        turned = pltpu.roll(kinds_t[low:high], (FIRST_O - KINDS * i) % CHANNELS, 1)
        wide = jnp.broadcast_to(turned[:, FIRST_O : FIRST_O + 1], (high - low, CHANNELS))
        masked = jnp.where(wide > 0, state[i, low:high], 0.0)
        state[i, low:high] = jnp.where(organic, turned, masked)

    for i in range(ROWS_DEV):
        if i < HALO or i >= ROWS_DEV - HALO:
            carry(i, 0, COLS_PAD)
        else:
            carry(i, LEFT, LEFT + 8)
            carry(i, 88, COLS_PAD)

    lane_free = lane_in >= FIRST_O + 5

    def turn_by(value, shift):
        return pltpu.roll(value, shift % CHANNELS, 1)

    def pack_state(cells):
        return [
            jnp.where(lane_free, turn_by(cells[3], FIRST_O + 5 - 20 * n), cells[n]) for n in range(3)
        ]

    def unpack_state(sent_cells):
        last = [turn_by(sent_cells[n], 20 * n - FIRST_O - 5) for n in range(3)]
        last = jnp.where(lane_in < 20, last[0], jnp.where(lane_in < 40, last[1], last[2]))
        return list(sent_cells) + [last]

    first_part = FIRST_O + TRACERS - 2 * ORGANIC

    def pack_organic(cells):
        others = jnp.where(
            lane_in >= first_part - FIRST_O,
            turn_by(cells[1], -ORGANIC),
            turn_by(cells[2], -FIRST_O),
        )
        return [jnp.where(organic, cells[0], others)]

    def pack_bars(cells):
        second = jnp.where(organic, turn_by(cells[3], FIRST_O - ORGANIC), cells[1])
        return [
            jnp.where(organic, turn_by(cells[3], FIRST_O), cells[0]),
            jnp.where(lane_in >= first_part, cells[2], second),
            jnp.where(organic, cells[3], cells[2]),
        ]

    def unpack_bars(sent_cells, early):
        third = jnp.where(organic, turn_by(early, FIRST_O), sent_cells[2])
        last = jnp.where(
            lane_in < ORGANIC,
            turn_by(sent_cells[0], -FIRST_O),
            turn_by(sent_cells[1], ORGANIC - FIRST_O),
        )
        return [
            jnp.where(organic, early, sent_cells[0]),
            jnp.where(organic, turn_by(early, ORGANIC), sent_cells[1]),
            jnp.where(lane_in >= first_part, sent_cells[1], third),
            jnp.where(organic, sent_cells[2], last),
        ]

    def received_cols(phase, side):
        cells = [col_in[phase, side, n] for n in range(3)]
        if phase == 0:
            return unpack_state(cells)
        return unpack_bars(cells, col_in[1, side, 0])

    def received_rows(phase, which, jj):
        cells = [row_in[phase, which, n, blocked(jj), :] for n in range(3)]
        if phase == 0:
            return unpack_state(cells)
        return unpack_bars(cells, row_in[1, which, 0, blocked(jj), :])

    def message(phase, which):
        move = MOVES[which]
        sent_rows = pl.ds(0, SENT[phase])
        if which < 2:
            source = row_out.at[phase, which, sent_rows, inner, :]
            target = row_in.at[phase, which, sent_rows, inner, :]
        elif which < 4:
            source = col_out.at[phase, which - 2, sent_rows]
            target = col_in.at[phase, which - 2, sent_rows]
        else:
            source, target = corner_out.at[phase, which - 4], corner_in.at[phase, which - 4]
        return pltpu.make_async_remote_copy(
            src_ref=source,
            dst_ref=target,
            send_sem=send_sem.at[phase, which],
            recv_sem=recv_sem.at[phase, which],
            device_id=(lat + move[0], lon + move[1]),
            device_id_type=MESH,
        )

    def send(phase, which):
        @pl.when(there(MOVES[which]))
        def _():
            message(phase, which).start()

    def sent(phase, which):
        @pl.when(there(MOVES[which]))
        def _():
            message(phase, which).wait_send()

    def arrived(phase, which):
        @pl.when(back(MOVES[which]))
        def _():
            message(phase, which).wait_recv()

    def corner_cells(which, inside):
        down, right = MOVES[4 + which]
        at = 0
        for depth in range(3):
            for t in range(3 - depth):
                if inside:
                    row = depth if down < 0 else ROWS_DEV - 1 - depth
                    column = LEFT + t if right < 0 else RIGHT - 1 - t
                else:
                    row = ROWS_DEV + depth if down < 0 else -1 - depth
                    column = RIGHT + t if right < 0 else LEFT - 1 - t
                yield at, row, column
                at += 1

    weight_cells = weights.reshape(5 * ALL_ROWS * COLS_PAD, CHANNELS)

    def column_cells(jj, s, base=0):
        return pl.ds(base + HALO * COLS_PAD + 8 * jj + s, ROWS_DEV, stride=COLS_PAD)

    def unpack_cols(phase, field):
        cells = field.reshape(ALL_ROWS * COLS_PAD, CHANNELS)
        for side in range(2):
            halo = received_cols(phase, side)
            for t in range(HALO):
                jj, s = cell(RIGHT + t if side == 0 else LEFT - HALO + t)
                cells[column_cells(jj, s), :] = halo[t]
                for k in range(5 if phase == 0 else 0):
                    weight_cells[column_cells(jj, s, k * ALL_ROWS * COLS_PAD), :] = (
                        jnp.broadcast_to(
                            halo[t][:, FIRST_O + k : FIRST_O + k + 1], (ROWS_DEV, CHANNELS)
                        )
                    )

    def unpack_rows(phase, field):
        for which in range(2):
            first = ALL_ROWS - HALO if which == 0 else 0
            for jj in range(BLOCKS):
                for r, cells in enumerate(received_rows(phase, which, jj)):
                    field[first + r, jj] = cells

        for which in range(4):
            for at, row, column in corner_cells(which, False):
                jj, s = cell(column)
                field[HALO + row, jj, s : s + 1, :] = corner_in[phase, which, at : at + 1, :]

    state_cells = state.reshape(ROWS_DEV * COLS_PAD, CHANNELS)
    for side in range(2):
        at = LEFT if side == 0 else RIGHT - HALO
        cells = [state_cells[pl.ds(at + t, ROWS_DEV, stride=COLS_PAD), :] for t in range(HALO)]
        for n, value in enumerate(pack_state(cells)):
            col_out[0, side, n] = value
    for which in range(2):
        first = 0 if which == 0 else ROWS_DEV - HALO
        for n, value in enumerate(pack_state([state[first + r] for r in range(HALO)])):
            row_out[0, which, n] = value

    for which in range(4):
        for at, row, column in corner_cells(which, True):
            corner_out[0, which, at : at + 1] = state[row, column : column + 1]

    order = (2, 3, 0, 1, 4, 5, 6, 7)
    pl.semaphore_wait(barrier, count)
    for which in order:
        send(0, which)

    v0 = v.at[0]

    lane_f = lane_in.astype(F32)
    upper = lane < TRACERS

    for load in loads[5:]:
        load.wait()
    vectors[...] = jnp.zeros_like(vectors)
    pieces[...] = jnp.zeros_like(pieces)
    for l in range(LEVELS):
        n, p, o = l * TRACERS, l * TRACERS + FIRST_P, l * TRACERS + FIRST_O
        end = (l + 1) * TRACERS
        vectors[0:1, p:o] = growth[...]
        vectors[1:2, p:o] = mortality[...]
        vectors[2:3, p:o] = sinking[...]
        vectors[3:4, o:end] = remineral[...]
        pieces[0, n : n + NUTRIENTS, p:o] = stoich[...]
        pieces[1, o:end, p:o] = routing[...]
        pieces[2, n : n + NUTRIENTS, o:end] = release[...]
        pieces[3, n : n + NUTRIENTS, p:o] = half_sat[...]
    rate, lost, sunk, decayed = (vectors[n : n + 1, :] for n in range(4))

    row_lane = lax.broadcasted_iota(jnp.int32, (CHANNELS, CHANNELS), 0)
    col_lane = lax.broadcasted_iota(jnp.int32, (CHANNELS, CHANNELS), 1)
    same = (row_lane < TRACERS) == (col_lane < TRACERS)
    row_in_level = lax.rem(row_lane, TRACERS)
    col_in_level = lax.rem(col_lane, TRACERS)
    row_p = (row_in_level >= FIRST_P) & (row_in_level < FIRST_O)
    col_p = (col_in_level >= FIRST_P) & (col_in_level < FIRST_O)
    own = jnp.where(row_lane == col_lane, 1.0, 0.0)
    own_p = jnp.where((row_lane == col_lane) & col_p, 1.0, 0.0)
    below = jnp.where(row_lane == col_lane + TRACERS, 1.0, 0.0)
    bars = own * ((1.0 - lost) * (1.0 - sunk) * (1.0 - decayed))
    bars += below * ((1.0 - lost) * sunk) + pieces[1] * lost + pieces[2] * decayed
    light = jnp.where(upper, 1.0, 0.4)
    drives = light * (own_p * (1.0 - sunk) + below * sunk - pieces[0])
    ones = jnp.where(col_p[0:1], 0.0, 1.0)
    halves_of = [pieces[3, k : k + 1, :] + pieces[3, TRACERS + k : TRACERS + k + 1, :] + ones for k in range(NUTRIENTS)]
    pick = jnp.where(same & (row_in_level < NUTRIENTS) & col_p, 1.0, 0.0).astype(BF16)
    collect = jnp.where(same & (col_in_level < NUTRIENTS) & row_p, 1.0, 0.0).astype(BF16)
    pick = jnp.concatenate([pick, pick], axis=0)
    collect = jnp.concatenate([collect, collect], axis=0)
    maps = jnp.concatenate([bars, drives], axis=1)
    maps_high = maps.astype(BF16)
    maps_low = (maps - maps_high.astype(F32)).astype(BF16)
    maps_twice = jnp.concatenate([maps_high, maps_high], axis=0)

    for i in range(HALO, ROWS_DEV - HALO):
        turned = pltpu.roll(kinds_t[16:88], (FIRST_O - KINDS * i) % CHANNELS, 1)
        state[i, 16:88] = jnp.where(organic, turned, state[i, 16:88])
    spread = jnp.concatenate(
        [jnp.where(row_lane == FIRST_O + k, 1.0, 0.0).astype(BF16) for k in range(5)], axis=1
    )
    spread = jnp.concatenate([spread, spread], axis=0)

    @pl.loop(0, GROUPS)
    def _(g):
        block = jnp.concatenate(
            [state[GROUP * g + r, blocked(jj), :] for r in range(GROUP) for jj in range(BLOCKS)],
            axis=0,
        )
        wide = dot(split(block), spread)
        for k in range(5):
            part = wide[:, CHANNELS * k : CHANNELS * (k + 1)]
            weights[k, pl.ds(HALO + GROUP * g, GROUP)] = part.reshape((GROUP,) + ROW)
        for r in range(GROUP):
            i = GROUP * g + r
            for jj in range(BLOCKS):
                cells = state[i, blocked(jj), :]
                v0[HALO + i, jj] = jnp.where(weights[0, HALO + i, jj] > 0, cells, 0.0)
                code = jnp.broadcast_to(cells[:, FIRST_O + 5 : FIRST_O + 6], (8, CHANNELS))
                second = jnp.floor((code + 0.5) * (1.0 / CODES))
                here = jnp.where(upper, code - CODES * second, second)
                hot[i, jj] = jnp.where(here == lane_f, 1.0, 0.0)
                halved = jnp.ones((8, CHANNELS), F32)
                for k in range(NUTRIENTS):
                    halved = jnp.where(here == k, halves_of[k], halved)
                halves[i, jj] = halved

    loads[4].wait()

    @pl.loop(0, GROUPS)
    def _(g):
        block = jnp.concatenate(
            [cot[GROUP * g + r, blocked(jj), :] for r in range(GROUP) for jj in range(BLOCKS)],
            axis=0,
        )
        parts = split(block)
        cells = pl.ds(pl.multiple_of(GROUP_CELLS * g, 8), GROUP_CELLS)
        both = dot(parts, maps_twice) + dot(parts[:, 0:CHANNELS], maps_low)
        bar0[cells] = both[:, :CHANNELS]
        drive[cells] = both[:, CHANNELS:]

    for side in range(2):
        cells = []
        for t in range(HALO):
            jj, s = cell(LEFT + t if side == 0 else RIGHT - HALO + t)
            cells.append(bar0[pl.ds(8 * jj + s, ROWS_DEV, stride=COLS_PAD), :])
        for n, value in enumerate(pack_organic(cells)):
            col_out[1, side, n] = value
    for which in range(2):
        first = 0 if which == 0 else ROWS_DEV - HALO
        for jj in range(BLOCKS):
            cells = [
                bar0[COLS_PAD * (first + r) + 8 * jj : COLS_PAD * (first + r) + 8 * jj + 8]
                for r in range(HALO)
            ]
            for n, value in enumerate(pack_organic(cells)):
                row_out[1, which, n, blocked(jj), :] = value
    for which in range(4):
        send(1, which)

    def inner_rows(block, to, src, step):
        count = (ROWS_DEV - 2 * step) // INNER_LOOPS[step]

        @pl.loop(0, INNER_LOOPS[step])
        def _(n):
            block(weights, to, src, HALO + step + count * n, count)

    one = (COLS_PAD, CHANNELS)

    def row_cells(r):
        return pl.ds(COLS_PAD * r if isinstance(r, int) else pl.multiple_of(COLS_PAD * r, 8), COLS_PAD)

    def pick_rows(rows):
        moved = [v[SUBSTEPS, HALO + r].reshape(one) * hot[r].reshape(one) for r in rows]
        chosen = dot(split(jnp.concatenate(moved, axis=0)), pick)
        for n, r in enumerate(rows):
            picked[row_cells(r)] = chosen[COLS_PAD * n : COLS_PAD * (n + 1)]

    def uptake_row(r):
        cells = row_cells(r)
        p = v[SUBSTEPS, HALO + r].reshape(one)
        halved = halves[r].reshape(one)
        force = drive[cells]
        chosen = picked[cells]
        total = chosen + halved
        inverse = pl.reciprocal(total, approx=True)
        inverse = inverse * (2.0 - total * inverse)
        return cells, p, halved, force, inverse, force * (chosen * inverse)

    def growth_rows(rows, add, spread):
        for n, r in enumerate(rows):
            near = slice(COLS_PAD * n, COLS_PAD * (n + 1))
            cells, p, halved, force, inverse, taken = uptake_row(r)
            if add:
                acc[...] += jnp.sum((taken * p).reshape(ROW), axis=0)
            if spread:
                pull[near] = (rate * force) * p * halved * (inverse * inverse)
                b[0, HALO + r] = (bar0[cells] + rate * taken).reshape(ROW)
        if spread:
            pulled = dot(split(pull[0 : COLS_PAD * len(rows)]), collect)
            for n, r in enumerate(rows):
                part = pulled[COLS_PAD * n : COLS_PAD * (n + 1)]
                b[0, HALO + r] += part.reshape(ROW) * hot[r]

    outer = list(range(HALO)) + list(range(ROWS_DEV - HALO, ROWS_DEV))

    for which in (2, 3):
        arrived(0, which)
    unpack_cols(0, v0)
    for step in range(1, SUBSTEPS + 1):
        inner_rows(forward_block, v.at[step], v.at[step - 1], step)
    acc[...] = jnp.zeros_like(acc)

    @pl.loop(1, GROUPS - 1)
    def _(g):
        rows = [GROUP * g + r for r in range(GROUP)]
        pick_rows(rows)
        growth_rows(rows, True, False)

    for which in (0, 1, 4, 5, 6, 7):
        arrived(0, which)
    unpack_rows(0, v0)

    halo_rows = list(range(HALO)) + list(range(ALL_ROWS - HALO, ALL_ROWS))
    wide = dot(split(jnp.concatenate([v0[i].reshape(one) for i in halo_rows], axis=0)), spread)
    for n, i in enumerate(halo_rows):
        for k in range(5):
            part = wide[COLS_PAD * n : COLS_PAD * (n + 1), CHANNELS * k : CHANNELS * (k + 1)]
            weights[k, i] = part.reshape(ROW)

    for step in range(1, SUBSTEPS + 1):
        outer_rows(forward_block, weights, v.at[step], v.at[step - 1], step)

    pick_rows(outer)
    growth_rows(outer, True, True)

    def exchange(stage, turn, slot):
        return pltpu.make_async_remote_copy(
            src_ref=gather.at[stage, slot],
            dst_ref=gather.at[stage, slot],
            send_sem=gsend_sem.at[stage, turn],
            recv_sem=grecv_sem.at[stage, slot],
            device_id=peer(stage, turn)[1],
            device_id_type=MESH,
        )

    def stage_start(stage, value):
        gather[stage, places[stage]] = value

        @pl.loop(1, NEAR)
        def _(turn):
            exchange(stage, turn, places[stage]).start()

    def stage_end(stage):
        @pl.loop(1, NEAR)
        def _(turn):
            exchange(stage, turn, peer(stage, turn)[0]).wait_recv()
            exchange(stage, turn, places[stage]).wait_send()

        parts = [gather[stage, n] for n in range(NEAR)]
        while len(parts) > 1:
            parts = [a + c for a, c in zip(parts[0::2], parts[1::2])]
        return parts[0]

    stage_start(0, jnp.sum(acc[...], axis=0, keepdims=True))
    b0 = b.at[0]
    for which in range(4):
        for at, row, column in corner_cells(which, True):
            jj, s = cell(column)
            corner_out[2, which, at : at + 1, :] = b0[HALO + row, jj, s : s + 1, :]
    for which in range(2):
        first = HALO if which == 0 else ROWS_DEV
        for jj in range(BLOCKS):
            cells = [b0[first + r, jj] for r in range(HALO)]
            for n, value in enumerate(pack_bars(cells)):
                row_out[2, which, n, blocked(jj), :] = value
    for which in (0, 1, 4, 5, 6, 7):
        send(2, which)

    @pl.loop(1, GROUPS - 1)
    def _(g):
        growth_rows([GROUP * g + r for r in range(GROUP)], False, True)

    b0_cells = b0.reshape(ALL_ROWS * COLS_PAD, CHANNELS)
    for side in range(2):
        cells = []
        for t in range(HALO):
            jj, s = cell(LEFT + t if side == 0 else RIGHT - HALO + t)
            cells.append(b0_cells[column_cells(jj, s), :])
        for n, value in enumerate(pack_bars(cells)):
            col_out[2, side, n] = value
    for which in (2, 3):
        send(2, which)

    def finish(i, jj, total):
        result[i - HALO, blocked(jj), :] = jnp.where(weights[0, i, jj] > 0, total, 0.0)

    goals = [into(b.at[step]) for step in range(1, SUBSTEPS)] + [finish]
    stage_start(1, stage_end(0))
    for which in (2, 3):
        arrived(1, which)
        arrived(2, which)
    unpack_cols(2, b0)
    for step in range(1, SUBSTEPS + 1):
        inner_rows(backward_block, goals[step - 1], b.at[step - 1], step)
    for which in (0, 1):
        arrived(1, which)
    for which in (0, 1, 4, 5, 6, 7):
        arrived(2, which)
    unpack_rows(2, b0)
    for step in range(1, SUBSTEPS + 1):
        outer_rows(backward_block, weights, goals[step - 1], b.at[step - 1], step)
    for phase in range(3):
        for which in range(4 if phase == 1 else 8):
            sent(phase, which)
    totals[...] = stage_end(1)


def finish_kernel(result, totals, out, growth_out, growth, sem):
    count = ROWS_DEV // GROUPS
    copies = [
        pltpu.make_async_copy(
            result.at[pl.ds(count * n, count), pl.ds(LEFT, COLS_DEV), :],
            out.at[pl.ds(count * n, count)],
            sem.at[n],
        )
        for n in range(GROUPS)
    ]
    for copy in copies:
        copy.start()
    lanes = totals[...]
    lanes = (lanes + pltpu.roll(lanes, TRACERS, 1)) * (1.0 / CELLS)
    growth[...] = pltpu.roll(lanes, CHANNELS - FIRST_P, 1)[:, 0:PHYTO]
    copies.append(pltpu.make_async_copy(growth, growth_out, sem.at[GROUPS]))
    copies[GROUPS].start()
    for copy in copies:
        copy.wait()


def shards(
    tracer_state,
    limit_codes,
    center_weight,
    side_weights,
    growth,
    half_sat,
    stoich,
    mortality,
    sinking,
    routing,
    remineral,
    release,
    cotangent,
):
    hbm = pl.BlockSpec(memory_space=pltpu.HBM)
    vmem = pl.BlockSpec(memory_space=pltpu.VMEM)
    padded = (ROWS_DEV, COLS_PAD, CHANNELS)
    cells = (ROWS_DEV,) + ROW
    field = (ALL_ROWS,) + ROW
    halo_rows = (3, 2, 3, COLS_PAD, CHANNELS)
    operands = (
        tracer_state,
        cotangent,
        jnp.transpose(limit_codes, (1, 0, 2)),
        center_weight,
        jnp.transpose(side_weights, (1, 0, 2)),
        growth[None, :],
        mortality[None, :],
        sinking[None, :],
        remineral[None, :],
        half_sat,
        stoich,
        routing,
        release,
    )
    results = pl.pallas_call(
        kernel,
        out_shape=(
            pltpu.VMEM(padded, F32),
            pltpu.VMEM((1, CHANNELS), F32),
        ),
        in_specs=[hbm] * len(operands),
        out_specs=(vmem,) * 2,
        scratch_shapes=[
            pltpu.VMEM(padded, F32),
            pltpu.VMEM(padded, F32),
        ]
        + [pltpu.VMEM(operand.shape, operand.dtype) for operand in operands[2:]]
        + [
            pltpu.VMEM((CHANNELS, CHANNELS), F32),
            pltpu.VMEM((COLS_PAD, CHANNELS), F32),
            pltpu.VMEM((8, CHANNELS), F32),
            pltpu.VMEM((4, CHANNELS, CHANNELS), F32),
            pltpu.VMEM(cells, F32),
            pltpu.VMEM(cells, F32),
            pltpu.VMEM((ROWS_DEV * COLS_PAD, CHANNELS), F32),
            pltpu.VMEM((ROWS_DEV * COLS_PAD, CHANNELS), F32),
            pltpu.VMEM((ROWS_DEV * COLS_PAD, CHANNELS), F32),
            pltpu.VMEM((ROWS_DEV * COLS_PAD, CHANNELS), F32),
            pltpu.VMEM((5,) + field, F32),
            pltpu.VMEM((SUBSTEPS + 1,) + field, F32),
            pltpu.VMEM((SUBSTEPS,) + field, F32),
            pltpu.VMEM((8, CHANNELS), F32),
            pltpu.VMEM(halo_rows, F32),
            pltpu.VMEM(halo_rows, F32),
            pltpu.VMEM((3, 2, 3, ROWS_DEV, CHANNELS), F32),
            pltpu.VMEM((3, 2, 3, ROWS_DEV, CHANNELS), F32),
            pltpu.VMEM((3, 4, 8, CHANNELS), F32),
            pltpu.VMEM((3, 4, 8, CHANNELS), F32),
            pltpu.VMEM((2, NEAR, 1, CHANNELS), F32),
            pltpu.SemaphoreType.DMA((len(operands),)),
            pltpu.SemaphoreType.DMA((3, 8)),
            pltpu.SemaphoreType.DMA((3, 8)),
            pltpu.SemaphoreType.DMA((2, NEAR)),
            pltpu.SemaphoreType.DMA((2, NEAR)),
        ],
        compiler_params=pltpu.CompilerParams(
            collective_id=0, has_side_effects=True, vmem_limit_bytes=65500000
        ),
        cost_estimate=pl.CostEstimate(flops=10**9, bytes_accessed=3 * 10**6, transcendentals=0),
    )(*operands)
    state_grad, growth_grad = pl.pallas_call(
        finish_kernel,
        out_shape=(
            jax.ShapeDtypeStruct((ROWS_DEV, COLS_DEV, CHANNELS), F32),
            jax.ShapeDtypeStruct((1, PHYTO), F32),
        ),
        in_specs=[vmem] * 2,
        out_specs=(hbm, hbm),
        scratch_shapes=[
            pltpu.VMEM((1, PHYTO), F32),
            pltpu.SemaphoreType.DMA((GROUPS + 1,)),
        ],
        compiler_params=pltpu.CompilerParams(vmem_limit_bytes=32 * 1024 * 1024),
        cost_estimate=pl.CostEstimate(flops=10**8, bytes_accessed=10**6, transcendentals=0),
    )(*results)
    return (state_grad, growth_grad[0])


def solution(mesh):
    in_specs = (
        P("lat", "lon", None),
        P(None, "lat", "lon"),
        P("lat", "lon"),
        P(None, "lat", "lon"),
        P(),
        P(),
        P(),
        P(),
        P(),
        P(),
        P(),
        P(),
        P("lat", "lon", None),
    )
    out_specs = (P("lat", "lon", None), P())
    return jax.shard_map(shards, mesh=mesh, in_specs=in_specs, out_specs=out_specs, check_vma=False)
```
